256 devices in a mesh: wide: 128 (over z, x, y), narrow: 2 (over core).
Axes of the slice: x: 4, y: 4, z: 8, core: 2. Of those that a mesh axis runs over, the one named last changes fastest.
Arguments:
- particle_position: float32 [2048, 3, 256], P(('wide', 'narrow')), may hold values from -1 to 1
- particle_velocity: float32 [2048, 3, 256], P(('wide', 'narrow')), may hold values from -4 to 4
- inverse_mass: float32 [2048, 256], P(('wide', 'narrow')), may hold values from 0.5 to 2
- facet_geometry: float32 [256, 4, 7, 128], P('wide')
- boulder_pose: float32 [256, 16], P('wide')
- boulder_velocity: float32 [256, 6], P('wide'), may hold values from -6 to 6
- boulder_slot: int32 [256], replicated, may hold values from 0 to 255, as said below
- block_home: int32 [2048], replicated, may hold values from 0 to 2047, as said below
- pair_facet: int32 [49152], P(('wide', 'narrow')), may hold values from 0 to 1023, as said below
- pair_block: int32 [49152], P(('wide', 'narrow')), may hold values from 0 to 2047, as said below
- pair_active: int32 [49152], P(('wide', 'narrow')), may hold values 0 or 1
Outputs:
- new_velocity: float32 [2048, 3, 256], P(('wide', 'narrow'))
- boulder_motion: float32 [256, 6], P('wide')
The draws below stay inside these ranges and needn't reach their ends.
Inputs may be any that keep to these rules, and one draw needn't show every extreme that they name: `boulder_slot`: A permutation: each slot once. Slot s belongs to owner s // 2. `block_home`: A permutation: each storage row once. Storage row r lies on device r // 8 in the order of wide+narrow. `pair_facet`: the 192 pairs of each device come in 64 runs of 3 consecutive pairs; all pairs of a run name boulders of one owner, and the runs of one device name different owners, so no device names more than 3 facet blocks of one owner. Every pair names a particle block stored on the device that holds the pair: block_home[pair_block[i]] // 8 is that device.
All inputs are finite; a program needn't handle non-finite values. No bound on the sum of `pair_active` on one device may be relied on, other than what follows from the above.
Results may differ from the reference program's by a relative error of at most 0.0001.
Values sent between devices are 32-bit elements; how exact they have to be, the bound alone decides.
No kernel may reach another device: no remote copies, remote signals or barrier semaphores. Data moves between devices by JAX's collectives and lax.ppermute only.
A program may use at most 64 MiB of HBM per device.

```python
import math
import jax
import jax.numpy as jnp
from jax import lax

FB = 128
FBLK = 4
PB = 256
PBLK_DEV = 8
BOUL_DEV = 2
CAP = 3
RUNS = 64
PAIRS_DEV = 192
NPB = 2048
BOULDERS = 256
NPAIRS = 49152
N_WIDE = 128
DEVICES = 256


def boulder_order(key):
    return jax.random.permutation(jax.random.fold_in(key, 101), BOULDERS).astype(jnp.int32)


def block_order(key):
    return jax.random.permutation(jax.random.fold_in(key, 202), NPB).astype(jnp.int32)


def draw_boulder_slot(key, part):
    shared = boulder_order(key)
    return shared


def draw_block_home(key, part):
    shared = block_order(key)
    return shared


def draw_pair_facet(key, part):
    slot_of = boulder_order(key)
    key = jax.random.fold_in(key, 2)
    boulder_at = jnp.argsort(slot_of, stable=True).astype(jnp.int32)
    hot_key, order_key, local_key, block_key = jax.random.split(key, 4)
    hottest = jax.random.randint(hot_key, (), 0, N_WIDE)
    device_keys = jax.random.split(order_key, DEVICES)

    def shuffled(device_key):
        return jax.random.permutation(device_key, N_WIDE - 1).astype(jnp.int32)
    others = jax.vmap(shuffled)(device_keys)
    steps_away = jnp.concatenate([jnp.zeros((DEVICES, 1), jnp.int32), 1 + others[:, :RUNS - 1]], axis=1)
    run_owner = (hottest + steps_away) % N_WIDE
    local_index = jax.random.randint(local_key, (DEVICES, RUNS, CAP), 0, BOUL_DEV)
    block_index = jax.random.randint(block_key, (DEVICES, RUNS, CAP), 0, FBLK)
    slot_index = run_owner[:, :, None] * BOUL_DEV + local_index
    return (boulder_at[slot_index] * FBLK + block_index).reshape(NPAIRS).astype(jnp.int32)


def draw_pair_block(key, part):
    home_row = block_order(key)
    key = jax.random.fold_in(key, 4)
    spatial_at = jnp.argsort(home_row, stable=True).astype(jnp.int32)
    local_index = jax.random.randint(key, (DEVICES, PAIRS_DEV), 0, PBLK_DEV)
    storage = jnp.arange(DEVICES, dtype=jnp.int32)[:, None] * PBLK_DEV + local_index
    return spatial_at[storage].reshape(NPAIRS).astype(jnp.int32)


def draw_facet_geometry(key, part):
    key = jax.random.fold_in(key, 5)
    first_key, second_key, third_key, fourth_key = jax.random.split(key, 4)
    tile_shape = (BOULDERS, FBLK, FB)
    offset = 0.3 * jax.random.normal(first_key, (BOULDERS, FBLK, 3, FB), jnp.float32)
    height = jax.random.uniform(second_key, tile_shape, jnp.float32, -1.0, 1.0)
    turning = jax.random.uniform(third_key, tile_shape, jnp.float32, -math.pi, math.pi)
    radial = jnp.sqrt(jnp.maximum(1.0 - height * height, 0.0))
    normal = jnp.stack([radial * jnp.cos(turning), radial * jnp.sin(turning), height], axis=2)
    surface = jnp.exp(jax.random.uniform(fourth_key, tile_shape, jnp.float32, math.log(0.5), math.log(2.0)))
    return jnp.concatenate([offset, normal, surface[:, :, None, :]], axis=2)


def draw_boulder_pose(key, part):
    key = jax.random.fold_in(key, 6)
    first_key, second_key, third_key, fourth_key, fifth_key = jax.random.split(key, 5)
    center = jax.random.uniform(first_key, (BOULDERS, 3), jnp.float32, -1.0, 1.0)
    leading = jax.random.uniform(second_key, (BOULDERS,), jnp.float32, 0.5, 1.0)
    vector = jax.random.uniform(third_key, (BOULDERS, 3), jnp.float32, -0.5, 0.5)
    length = jnp.sqrt(leading * leading + jnp.sum(vector * vector, axis=1))
    a = leading / length
    b = vector[:, 0] / length
    c = vector[:, 1] / length
    d = vector[:, 2] / length
    rotation = jnp.stack([1 - 2 * (c * c + d * d), 2 * (b * c - a * d), 2 * (b * d + a * c), 2 * (b * c + a * d), 1 - 2 * (b * b + d * d), 2 * (c * d - a * b), 2 * (b * d - a * c), 2 * (c * d + a * b), 1 - 2 * (b * b + c * c)], axis=1)
    mass_inverse = jnp.exp(jax.random.uniform(fourth_key, (BOULDERS, 1), jnp.float32, math.log(0.001), math.log(0.004)))
    inertia_inverse = jnp.exp(jax.random.uniform(fifth_key, (BOULDERS, 3), jnp.float32, math.log(0.004), math.log(0.016)))
    return jnp.concatenate([center, rotation, mass_inverse, inertia_inverse], axis=1)


def with_ends(values, own_key, least, high):
    longest = values.shape.index(max(values.shape))
    spots = []
    for shift in (0, 1):
        where = [jax.random.randint(jax.random.fold_in(own_key, axis), (), 0, length) for axis, length in enumerate(values.shape)]
        where[longest] = (where[longest] + shift) % values.shape[longest]
        spots.append(tuple(where))
    return values.at[spots[0]].set(least).at[spots[1]].set(high)


def levels(key, extent, cuts, smallest, largest):
    level = 1.0
    for position, blocks in cuts:
        heights = jax.random.uniform(jax.random.fold_in(jax.random.fold_in(key, 6), position), (blocks,), jnp.float32, smallest / len(cuts), largest / len(cuts))
        level = level * jnp.repeat(jnp.exp(heights), extent[position] // blocks).reshape((-1,) + (1,) * (len(extent) - 1 - position))
    return level


def gaussian(stream_key, shape, width, limit, pieces=(), kind=jnp.bfloat16):
    drawn = width * jax.random.normal(stream_key, shape, jnp.float32)
    if pieces:
        drawn = drawn * levels(stream_key, shape, pieces, -0.22, 0.18)
    return jnp.clip(drawn, -limit, limit).astype(kind)


def setup_inputs(seed: int = 0) -> dict:
    arg_keys = jax.random.split(jax.random.key(seed), 12)
    particle_position = jnp.clip(jax.random.uniform(arg_keys[0], (NPB, 3, PB), jnp.float32, -1.0, 1.0) * levels(arg_keys[0], (NPB, 3, PB), ((0, 256),), -0.4, 0.0), -1.0, 1.0)
    particle_velocity = gaussian(arg_keys[1], (NPB, 3, PB), 0.3, 4.0, ((0, 256),), jnp.float32)
    inverse_mass = jnp.clip(jnp.exp(math.log(2.0) - 1.3862944 * jax.random.uniform(arg_keys[2], (NPB, PB), jnp.float32) ** levels(arg_keys[2], (NPB, PB), ((0, 256),), -0.2, 0.2)), 0.5, 2.0)
    facet_geometry = draw_facet_geometry(jax.random.fold_in(arg_keys[11], 71), 0)
    boulder_pose = draw_boulder_pose(jax.random.fold_in(arg_keys[11], 71), 0)
    boulder_velocity = gaussian(arg_keys[5], (BOULDERS, 6), 0.5, 6.0, ((0, 128),), jnp.float32)
    boulder_slot = draw_boulder_slot(jax.random.fold_in(arg_keys[11], 71), 0)
    block_home = draw_block_home(jax.random.fold_in(arg_keys[11], 71), 0)
    pair_facet = draw_pair_facet(jax.random.fold_in(arg_keys[11], 71), 0)
    pair_block = draw_pair_block(jax.random.fold_in(arg_keys[11], 71), 0)
    pair_active = with_ends((jax.random.randint(arg_keys[10], (NPAIRS,), 0, 4) < 3).astype(jnp.int32), jax.random.fold_in(arg_keys[10], 1), 0, 1)
    return {"particle_position": particle_position, "particle_velocity": particle_velocity, "inverse_mass": inverse_mass, "facet_geometry": facet_geometry, "boulder_pose": boulder_pose, "boulder_velocity": boulder_velocity, "boulder_slot": boulder_slot, "block_home": block_home, "pair_facet": pair_facet, "pair_block": pair_block, "pair_active": pair_active}


PENALTY = 0.3
SHARPNESS = 4.0
CONTACT_GAP = 0.1
TIME_STEP = 0.5


def rotate_parts(boulder_pose, parts):
    result = []
    for row_index in range(3):
        summed = boulder_pose[:, 3 + 3 * row_index][:, None, None] * parts[0]
        summed = summed + boulder_pose[:, 4 + 3 * row_index][:, None, None] * parts[1]
        summed = summed + boulder_pose[:, 5 + 3 * row_index][:, None, None] * parts[2]
        result.append(summed)
    return result


def world_facets(geometry, boulder_pose):
    lever_arm = rotate_parts(boulder_pose, [geometry[:, :, 0], geometry[:, :, 1], geometry[:, :, 2]])
    normal = rotate_parts(boulder_pose, [geometry[:, :, 3], geometry[:, :, 4], geometry[:, :, 5]])
    centroid = [boulder_pose[:, component][:, None, None] + lever_arm[component] for component in range(3)]
    world_facet = jnp.stack(centroid + normal + [geometry[:, :, 6]], axis=2)
    return world_facet, jnp.stack(lever_arm, axis=2)


def contact_tile(facet, points):
    offset = [points[component][None, :] - facet[component][:, None] for component in range(3)]
    distance = facet[3][:, None] * offset[0] + facet[4][:, None] * offset[1] + facet[5][:, None] * offset[2]
    square = offset[0] * offset[0] + offset[1] * offset[1] + offset[2] * offset[2]
    weight = jnp.exp(-square) * jax.nn.softplus(SHARPNESS * (CONTACT_GAP - distance)) / SHARPNESS
    facet_load = jnp.sum(weight, axis=1)
    pushed = facet[6][None, :] * facet[3:6]
    push_sum = jnp.dot(pushed, weight, precision=lax.Precision.HIGHEST)
    return PENALTY * push_sum, facet_load


def boulder_update(totals, world_facet, lever_arm, boulder_pose, boulder_velocity):
    scaled = -PENALTY * world_facet[:, :, 6] * totals
    push = [scaled * world_facet[:, :, 3 + component] for component in range(3)]
    force_sum = [jnp.sum(push[component], axis=(1, 2)) for component in range(3)]
    torque = [
        jnp.sum(lever_arm[:, :, 1] * push[2] - lever_arm[:, :, 2] * push[1], axis=(1, 2)),
        jnp.sum(lever_arm[:, :, 2] * push[0] - lever_arm[:, :, 0] * push[2], axis=(1, 2)),
        jnp.sum(lever_arm[:, :, 0] * push[1] - lever_arm[:, :, 1] * push[0], axis=(1, 2)),
    ]
    body_torque = []
    for column_index in range(3):
        summed = boulder_pose[:, 3 + column_index] * torque[0]
        summed = summed + boulder_pose[:, 6 + column_index] * torque[1]
        summed = summed + boulder_pose[:, 9 + column_index] * torque[2]
        body_torque.append(summed * boulder_pose[:, 13 + column_index])
    angular = []
    for row_index in range(3):
        summed = boulder_pose[:, 3 + 3 * row_index] * body_torque[0]
        summed = summed + boulder_pose[:, 4 + 3 * row_index] * body_torque[1]
        summed = summed + boulder_pose[:, 5 + 3 * row_index] * body_torque[2]
        angular.append(boulder_velocity[:, 3 + row_index] + TIME_STEP * summed)
    linear = [boulder_velocity[:, component] + TIME_STEP * boulder_pose[:, 12] * force_sum[component] for component in range(3)]
    return jnp.stack(linear + angular, axis=1)


def reference(particle_position, particle_velocity, inverse_mass, facet_geometry, boulder_pose, boulder_velocity, boulder_slot, block_home, pair_facet, pair_block, pair_active):
    world_facet, lever_arm = world_facets(facet_geometry, boulder_pose)
    facet_count = world_facet.shape[-1]
    world_flat = world_facet.reshape(BOULDERS * FBLK, 7, facet_count)
    facet_row = (boulder_slot[pair_facet // FBLK] * FBLK + pair_facet % FBLK).astype(jnp.int32)
    block_row = block_home[pair_block].astype(jnp.int32)
    active = pair_active.astype(jnp.float32)

    def one_device(carry, members):
        force_sum, load_sum = carry
        rows_facet, rows_block, flags = members
        facets = world_flat[rows_facet]
        points = particle_position[rows_block]
        pushes, loads = jax.vmap(contact_tile)(facets, points)
        force_sum = force_sum.at[rows_block].add(pushes * flags[:, None, None])
        load_sum = load_sum.at[rows_facet].add(loads * flags[:, None])
        return (force_sum, load_sum), None

    start = (jnp.zeros(particle_position.shape, jnp.float32), jnp.zeros((BOULDERS * FBLK, facet_count), jnp.float32))
    members = (facet_row.reshape(DEVICES, PAIRS_DEV), block_row.reshape(DEVICES, PAIRS_DEV), active.reshape(DEVICES, PAIRS_DEV))
    (force_sum, load_sum), unused = lax.scan(one_device, start, members)
    new_velocity = particle_velocity + TIME_STEP * inverse_mass[:, None, :] * force_sum
    totals = load_sum.reshape(BOULDERS, FBLK, facet_count)
    boulder_motion = boulder_update(totals, world_facet, lever_arm, boulder_pose, boulder_velocity)
    return new_velocity, boulder_motion
```

```python
import functools

import jax
import jax.numpy as jnp
from jax import lax
from jax.experimental import pallas as pl
from jax.experimental.pallas import tpu as pltpu
from jax.sharding import PartitionSpec as P

PENALTY = 0.3
SHARPNESS = 4.0
CONTACT_GAP = 0.1
TIME_STEP = 0.5

PLANE = 16
DEPTH = 8
BLOCKS = 8
TERMS = 32
FACETS = PLANE * BLOCKS
PARTICLES = DEPTH * BLOCKS
UNROLL = 2
VMEM_LIMIT = 48 * 1024 * 1024

F32 = jnp.float32
BF16 = jnp.bfloat16


def split3(value):
    high = value.astype(BF16).astype(F32)
    rest = value - high
    middle = rest.astype(BF16).astype(F32)
    return high, middle, (rest - middle).astype(BF16).astype(F32)


def facet_message(geometry_ref, pose_ref, out_ref):
    lane = lax.broadcasted_iota(jnp.int32, (4, 128), 1)
    for boulder in range(2):
        part = [geometry_ref[boulder, :, row, :] for row in range(7)]
        center = [pose_ref[boulder, row] for row in range(3)]
        rotation = [pose_ref[boulder, 3 + entry] for entry in range(9)]
        rows = []
        for first in (0, 3):
            for row in range(3):
                rows.append(
                    rotation[3 * row] * part[first]
                    + rotation[3 * row + 1] * part[first + 1]
                    + rotation[3 * row + 2] * part[first + 2]
                )
        rows.append(part[6])
        rows.append(
            jnp.where(
                lane == 0,
                center[0],
                jnp.where(lane == 1, center[1], jnp.where(lane == 2, center[2], 0.0)),
            )
        )
        for target in range(PLANE):
            for row in range(8):
                out_ref[target, row, 4 * boulder : 4 * boulder + 4, :] = rows[row]


def pair_message(
    position_ref, slot_ref, home_ref, facet_ref, block_ref, active_ref, out_ref, keep_ref
):
    pairs = facet_ref.shape[0]
    lane = lax.broadcasted_iota(jnp.int32, (pairs, 128), 1)

    def look_up(table, index):
        rows = table.shape[0]
        row = lax.broadcasted_iota(jnp.int32, (pairs, rows), 1)
        onehot = ((index >> 7) == row).astype(F32).astype(BF16)
        picked = jnp.dot(onehot, table.astype(F32).astype(BF16), preferred_element_type=F32)
        picked = jnp.where(lane == (index & 127), picked, 0.0)
        return jnp.sum(picked, axis=1, keepdims=True).astype(jnp.int32)

    facet = facet_ref[...]
    slot = look_up(slot_ref[...], facet >> 2)
    local_block = look_up(home_ref[...] & 7, block_ref[...])
    plane = slot >> 5
    code = local_block * 256 + ((slot & 31) * 4 + (facet & 3))
    code = code.astype(F32)
    active = active_ref[...] != 0
    member = jnp.logical_and(lane == plane, active).astype(F32)
    row = lax.broadcasted_iota(jnp.int32, (pairs, pairs), 0)
    column = lax.broadcasted_iota(jnp.int32, (pairs, pairs), 1)
    below = (column < row).astype(F32).astype(BF16)
    before = jnp.dot(below, member.astype(BF16), preferred_element_type=F32)
    rank = jnp.sum(before * member, axis=1, keepdims=True).astype(jnp.int32)
    rank = jnp.where(active, rank, 255)
    spread = jnp.where(lane == rank, code, 0.0)
    lane_row = lax.broadcasted_iota(jnp.int32, (1, 128), 1)
    for part in range(3):
        keep_ref[8 * part : 8 * part + 8, :] = position_ref[:, part, :]
    near = keep_ref[:, 0:128]
    far = keep_ref[:, 128:256]
    for target in range(DEPTH):
        here = jnp.logical_and(plane == target, active)
        listed = jnp.sum(jnp.where(here, spread, 0.0), axis=0, keepdims=True)
        count = jnp.sum(here.astype(F32), axis=0, keepdims=True)
        listed = jnp.where(lane_row == 127, count, listed)
        out_ref[target, 0:24, :] = near
        out_ref[target, 24:48, :] = far
        out_ref[target, 48:56, :] = jnp.broadcast_to(listed, (8, 128))


def facet_features(world_ref, terms_ref, push_ref, terms_keep, push_keep):
    terms_keep[...] = jnp.zeros(terms_keep.shape, F32)
    push_keep[...] = jnp.zeros(push_keep.shape, F32)

    def owner(index, carry):
        lever = [world_ref[index, part] for part in range(3)]
        normal = [world_ref[index, 3 + part] for part in range(3)]
        area = world_ref[index, 6]
        last = world_ref[index, 7]
        center = [lever[part] + last[:, part : part + 1] for part in range(3)]
        along = normal[0] * center[0] + normal[1] * center[1] + normal[2] * center[2]
        square = center[0] * center[0] + center[1] * center[1] + center[2] * center[2]
        sides = (
            ([-SHARPNESS * value for value in normal], SHARPNESS * (CONTACT_GAP + along), 0.0),
            ([2.0 * value for value in center], -square, 1.0),
        )
        for side, (factors, constant, tail) in enumerate(sides):
            split = [split3(value) for value in factors]
            order = (0, 1, 2, 0, 1, 0)
            for group, level in enumerate(order):
                for part in range(3):
                    terms_keep[side * TERMS + 3 * group + part] = split[part][level]
            for level, value in enumerate(split3(constant)):
                terms_keep[side * TERMS + 18 + level] = value
                terms_keep[side * TERMS + 21 + level] = jnp.full((8, 128), tail, F32)
        scaled = (PENALTY / SHARPNESS) * area
        push = [scaled * value for value in normal]
        push.append(lever[1] * push[2] - lever[2] * push[1])
        push.append(lever[2] * push[0] - lever[0] * push[2])
        push.append(lever[0] * push[1] - lever[1] * push[0])
        for part in range(6):
            high = push[part].astype(BF16).astype(F32)
            push_keep[part] = high
            push_keep[8 + part] = push[part] - high
        for block in range(BLOCKS):
            both = terms_keep[:, block, :]
            terms_ref[index * BLOCKS + block, 0:128, :] = both[:TERMS].T.astype(BF16)
            terms_ref[index * BLOCKS + block, 128:256, :] = both[TERMS:].T.astype(BF16)
            push_ref[index * BLOCKS + block] = push_keep[:, block, :].astype(BF16)
        return carry

    lax.fori_loop(0, PLANE, owner, 0)
    terms_ref[FACETS] = jnp.zeros((256, TERMS), BF16)
    push_ref[FACETS] = jnp.zeros((16, 128), BF16)


def contact(
    terms_ref, push_ref, given_ref, force_ref, load_ref,
    table, listed, point_keep, points, force_sum, load_sum, sem,
):
    copy = pltpu.make_async_copy(given_ref.at[:, pl.ds(48, 8), :], table, sem)
    copy.start()
    point_keep[...] = jnp.zeros(point_keep.shape, F32)
    force_sum[...] = jnp.zeros(force_sum.shape, F32)
    load_sum[...] = jnp.zeros(load_sum.shape, F32)
    points[PARTICLES] = jnp.zeros((TERMS, 256), BF16)

    def source(index, carry):
        for half in range(2):
            lanes = slice(128 * half, 128 * half + 128)
            place = [
                given_ref[index, 24 * half + 8 * part : 24 * half + 8 * part + 8, :]
                for part in range(3)
            ]
            square = place[0] * place[0] + place[1] * place[1] + place[2] * place[2]
            split = [split3(value) for value in place]
            for group, level in enumerate((0, 0, 0, 1, 1, 2)):
                for part in range(3):
                    point_keep[3 * group + part, :, lanes] = split[part][level]
            for level, value in enumerate(split3(-square)):
                point_keep[18 + level, :, lanes] = jnp.full((8, 128), 1.0, F32)
                point_keep[21 + level, :, lanes] = value
        for block in range(BLOCKS):
            points[index * BLOCKS + block] = point_keep[:, block, :].astype(BF16)
        return carry

    lax.fori_loop(0, DEPTH, source, 0)
    copy.wait()

    def gather(index, start):
        count = table[index, 0, 127].astype(jnp.int32)
        shift = index * (BLOCKS * 256)

        def entry(place, carry):
            listed[start + place] = table[index, 0, place].astype(jnp.int32) + shift
            return carry

        lax.fori_loop(0, count, entry, 0)
        return start + count

    total = lax.fori_loop(0, DEPTH, gather, 0)
    for spare in range(UNROLL):
        listed[total + spare] = PARTICLES * 256 + FACETS

    def step(index, carry):
        done = []
        for lane in range(UNROLL):
            code = listed[index * UNROLL + lane]
            block = code >> 8
            facet = code & 255
            both = jnp.dot(terms_ref[facet], points[block], preferred_element_type=F32)
            gap = both[:128]
            soft = jnp.where(gap > 80.0, gap, jnp.log(1.0 + jnp.exp(gap)))
            weight = jnp.exp(both[128:]) * soft
            high = weight.astype(BF16)
            low = (weight - high.astype(F32)).astype(BF16)
            push = push_ref[facet]
            result = jnp.dot(push, high, preferred_element_type=F32) + jnp.dot(
                push, low, preferred_element_type=F32
            )
            done.append((block, facet >> 2, result[0:8] + result[8:16]))
        for block, boulder, result in done:
            force_sum[block] += result
            load_sum[boulder] += result[:, :128] + result[:, 128:]
        return carry

    lax.fori_loop(0, (total + UNROLL - 1) // UNROLL, step, 0)
    for index in range(DEPTH):
        for block in range(BLOCKS):
            force_ref[index, 3 * block : 3 * block + 3, :] = force_sum[
                index * BLOCKS + block, 0:3, :
            ]
    load_ref[...] = load_sum[0 : 2 * PLANE]


def finish_particles(force_ref, velocity_ref, mass_ref, out_ref):
    total = force_ref[0]
    for index in range(1, DEPTH):
        total = total + force_ref[index]
    scaled = TIME_STEP * mass_ref[...]
    for block in range(BLOCKS):
        out_ref[block] = velocity_ref[block] + scaled[block : block + 1, :] * total[
            3 * block : 3 * block + 3, :
        ]


def sum_loads(load_ref, out_ref):
    total = load_ref[0]
    for index in range(1, PLANE):
        total = total + load_ref[index]
    out_ref[...] = total


def finish_boulders(own_ref, other_ref, pose_ref, velocity_ref, out_ref):
    row = lax.broadcasted_iota(jnp.int32, (2, 6), 0)
    column = lax.broadcasted_iota(jnp.int32, (2, 6), 1)
    change = jnp.zeros((2, 6), F32)
    for boulder in range(2):
        total = jnp.sum(own_ref[boulder] + other_ref[boulder], axis=1, keepdims=True)
        force = [-total[part : part + 1, :] for part in range(3)]
        torque = [-total[3 + part : 4 + part, :] for part in range(3)]
        moves = [pose_ref[boulder, 12] * value for value in force]
        body = []
        for part in range(3):
            turned = (
                pose_ref[boulder, 3 + part] * torque[0]
                + pose_ref[boulder, 6 + part] * torque[1]
                + pose_ref[boulder, 9 + part] * torque[2]
            )
            body.append(turned * pose_ref[boulder, 13 + part])
        for part in range(3):
            moves.append(
                pose_ref[boulder, 3 + 3 * part] * body[0]
                + pose_ref[boulder, 4 + 3 * part] * body[1]
                + pose_ref[boulder, 5 + 3 * part] * body[2]
            )
        for part in range(6):
            here = jnp.logical_and(row == boulder, column == part)
            change = change + jnp.where(here, moves[part], 0.0)
    out_ref[...] = velocity_ref[...] + TIME_STEP * change


VMEM = pl.BlockSpec(memory_space=pltpu.VMEM)
SMEM = pl.BlockSpec(memory_space=pltpu.SMEM)


def call(kernel, outs, in_specs, scratch=(), cost=None):
    single = not isinstance(outs, list)
    return pl.pallas_call(
        kernel,
        out_shape=outs,
        in_specs=in_specs,
        out_specs=VMEM if single else [VMEM] * len(outs),
        scratch_shapes=list(scratch),
        cost_estimate=cost,
        compiler_params=pltpu.CompilerParams(vmem_limit_bytes=VMEM_LIMIT),
    )


def shards(
    particle_position,
    particle_velocity,
    inverse_mass,
    facet_geometry,
    boulder_pose,
    boulder_velocity,
    boulder_slot,
    block_home,
    pair_facet,
    pair_block,
    pair_active,
):
    owners = lax.axis_size("wide")
    planes = [[PLANE * depth + spot for spot in range(PLANE)] for depth in range(owners // PLANE)]
    columns = [[PLANE * depth + spot for depth in range(DEPTH)] for spot in range(PLANE)]
    swap = functools.partial(
        lax.all_to_all, axis_name="wide", split_axis=0, concat_axis=0, tiled=True
    )
    pairs = pair_facet.shape[0]
    shape = jax.ShapeDtypeStruct

    facets = call(facet_message, shape((PLANE, 8, BLOCKS, 128), F32), [VMEM, SMEM])(
        facet_geometry, boulder_pose
    )
    facets = swap(facets, axis_index_groups=planes)
    particles = call(
        pair_message, shape((DEPTH, 56, 128), F32), [VMEM] * 6, [pltpu.VMEM((24, 256), F32)]
    )(
        particle_position,
        boulder_slot.reshape(2, 128),
        block_home.reshape(16, 128),
        pair_facet.reshape(pairs, 1),
        pair_block.reshape(pairs, 1),
        pair_active.reshape(pairs, 1),
    )
    particles = swap(particles, axis_index_groups=columns)
    terms, push = call(
        facet_features,
        [shape((FACETS + 1, 256, TERMS), BF16), shape((FACETS + 1, 16, 128), BF16)],
        [VMEM],
        [pltpu.VMEM((2 * TERMS, BLOCKS, 128), F32), pltpu.VMEM((16, BLOCKS, 128), F32)],
    )(facets)
    force, load = call(
        contact,
        [shape((DEPTH, 24, 256), F32), shape((2 * PLANE, 8, 128), F32)],
        [VMEM] * 3,
        [
            pltpu.SMEM((DEPTH, 8, 128), F32),
            pltpu.SMEM((DEPTH * 48 + UNROLL,), jnp.int32),
            pltpu.VMEM((TERMS, BLOCKS, 256), F32),
            pltpu.VMEM((PARTICLES + 1, TERMS, 256), BF16),
            pltpu.VMEM((PARTICLES + 1, 8, 256), F32),
            pltpu.VMEM((2 * PLANE + 1, 8, 128), F32),
            pltpu.SemaphoreType.DMA,
        ],
    )(terms, push, particles)
    load = swap(load, axis_index_groups=planes)
    load = call(sum_loads, shape((2, 8, 128), F32), [VMEM])(load.reshape(PLANE, 2, 8, 128))
    other = lax.ppermute(load, "narrow", [(0, 1), (1, 0)])
    boulder_motion = call(
        finish_boulders, shape(boulder_velocity.shape, F32), [VMEM, VMEM, SMEM, VMEM]
    )(load, other, boulder_pose, boulder_velocity)
    force = swap(force, axis_index_groups=columns)
    new_velocity = call(finish_particles, shape(particle_velocity.shape, F32), [VMEM] * 3)(
        force, particle_velocity, inverse_mass
    )
    return (new_velocity, boulder_motion)


def solution(mesh):
    return jax.shard_map(
        shards,
        mesh=mesh,
        in_specs=(
            P(("wide", "narrow"), None, None),
            P(("wide", "narrow"), None, None),
            P(("wide", "narrow"), None),
            P("wide", None, None, None),
            P("wide", None),
            P("wide", None),
            P(),
            P(),
            P(("wide", "narrow")),
            P(("wide", "narrow")),
            P(("wide", "narrow")),
        ),
        out_specs=(P(("wide", "narrow"), None, None), P("wide", None)),
        check_vma=False,
    )
```

```python
import functools

import jax
import jax.numpy as jnp
from jax import lax
from jax.experimental import pallas as pl
from jax.experimental.pallas import tpu as pltpu
from jax.sharding import PartitionSpec as P

PENALTY = 0.3
SHARPNESS = 4.0
CONTACT_GAP = 0.1
TIME_STEP = 0.5

PLANE = 16
DEPTH = 8
BLOCKS = 8
TERMS = 32
FACETS = PLANE * BLOCKS
PARTICLES = DEPTH * BLOCKS
GROUP = 2
VMEM_LIMIT = 24 * 1024 * 1024

F32 = jnp.float32
BF16 = jnp.bfloat16


def split3(value):
    high = value.astype(BF16).astype(F32)
    rest = value - high
    middle = rest.astype(BF16).astype(F32)
    return high, middle, (rest - middle).astype(BF16).astype(F32)


def facet_message(geometry_ref, pose_ref, out_ref):
    lane = lax.broadcasted_iota(jnp.int32, (4, 128), 1)
    for boulder in range(2):
        part = [geometry_ref[boulder, :, row, :] for row in range(7)]
        center = [pose_ref[boulder, row] for row in range(3)]
        rotation = [pose_ref[boulder, 3 + entry] for entry in range(9)]
        rows = []
        for first in (0, 3):
            for row in range(3):
                rows.append(
                    rotation[3 * row] * part[first]
                    + rotation[3 * row + 1] * part[first + 1]
                    + rotation[3 * row + 2] * part[first + 2]
                )
        rows.append(part[6])
        rows.append(
            jnp.where(
                lane == 0,
                center[0],
                jnp.where(lane == 1, center[1], jnp.where(lane == 2, center[2], 0.0)),
            )
        )
        for target in range(PLANE):
            for row in range(8):
                out_ref[target, row, 4 * boulder : 4 * boulder + 4, :] = rows[row]


def pair_message(
    position_ref, slot_ref, home_ref, facet_ref, block_ref, active_ref, out_ref
):
    pairs = facet_ref.shape[0]
    lane = lax.broadcasted_iota(jnp.int32, (pairs, 128), 1)

    def look_up(table, index):
        rows = table.shape[0]
        row = lax.broadcasted_iota(jnp.int32, (pairs, rows), 1)
        onehot = ((index >> 7) == row).astype(F32).astype(BF16)
        picked = jnp.dot(onehot, table.astype(F32).astype(BF16), preferred_element_type=F32)
        picked = jnp.where(lane == (index & 127), picked, 0.0)
        return jnp.sum(picked, axis=1, keepdims=True).astype(jnp.int32)

    facet = facet_ref[...]
    slot = look_up(slot_ref[...], facet >> 2)
    local_block = look_up(home_ref[...] & 7, block_ref[...])
    plane = slot >> 5
    code = local_block * 256 + ((slot & 31) * 4 + (facet & 3))
    code = code.astype(F32)
    active = active_ref[...] != 0
    member = jnp.logical_and(lane == plane, active).astype(F32)
    row = lax.broadcasted_iota(jnp.int32, (pairs, pairs), 0)
    column = lax.broadcasted_iota(jnp.int32, (pairs, pairs), 1)
    below = (column < row).astype(F32).astype(BF16)
    before = jnp.dot(below, member.astype(BF16), preferred_element_type=F32)
    rank = jnp.sum(before * member, axis=1, keepdims=True).astype(jnp.int32)
    rank = jnp.where(active, rank, 255)
    spread = jnp.where(lane == rank, code, 0.0)
    lane_row = lax.broadcasted_iota(jnp.int32, (1, 128), 1)
    for target in range(DEPTH):
        here = jnp.logical_and(plane == target, active)
        listed = jnp.sum(jnp.where(here, spread, 0.0), axis=0, keepdims=True)
        count = jnp.sum(here.astype(F32), axis=0, keepdims=True)
        listed = jnp.where(lane_row == 127, count, listed)
        for half in range(2):
            for part in range(3):
                first = 24 * half + 8 * part
                out_ref[target, first : first + 8, :] = position_ref[
                    part, :, 128 * half : 128 * half + 128
                ]
        out_ref[target, 48:56, :] = jnp.broadcast_to(listed, (8, 128))


def facet_features(world_ref, terms_ref, push_ref, terms_keep, push_keep):
    terms_keep[...] = jnp.zeros(terms_keep.shape, F32)
    push_keep[...] = jnp.zeros(push_keep.shape, F32)

    def owner(index, carry):
        lever = [world_ref[index, part] for part in range(3)]
        normal = [world_ref[index, 3 + part] for part in range(3)]
        area = world_ref[index, 6]
        last = world_ref[index, 7]
        center = [lever[part] + last[:, part : part + 1] for part in range(3)]
        along = normal[0] * center[0] + normal[1] * center[1] + normal[2] * center[2]
        square = center[0] * center[0] + center[1] * center[1] + center[2] * center[2]
        sides = (
            ([-SHARPNESS * value for value in normal], SHARPNESS * (CONTACT_GAP + along), 0.0),
            ([2.0 * value for value in center], -square, 1.0),
        )
        for side, (factors, constant, tail) in enumerate(sides):
            split = [split3(value) for value in factors]
            order = (0, 1, 2, 0, 1, 0)
            for group, level in enumerate(order):
                for part in range(3):
                    terms_keep[side * TERMS + 3 * group + part] = split[part][level]
            for level, value in enumerate(split3(constant)):
                terms_keep[side * TERMS + 18 + level] = value
                terms_keep[side * TERMS + 21 + level] = jnp.full((8, 128), tail, F32)
        scaled = (PENALTY / SHARPNESS) * area
        push = [scaled * value for value in normal]
        push.append(lever[1] * push[2] - lever[2] * push[1])
        push.append(lever[2] * push[0] - lever[0] * push[2])
        push.append(lever[0] * push[1] - lever[1] * push[0])
        for part in range(6):
            high = push[part].astype(BF16).astype(F32)
            push_keep[part] = high
            push_keep[8 + part] = push[part] - high
        for block in range(BLOCKS):
            both = terms_keep[:, block, :]
            terms_ref[index * BLOCKS + block, 0:128, :] = both[:TERMS].T.astype(BF16)
            terms_ref[index * BLOCKS + block, 128:256, :] = both[TERMS:].T.astype(BF16)
            push_ref[index * BLOCKS + block] = push_keep[:, block, :].astype(BF16)
        return carry

    lax.fori_loop(0, PLANE, owner, 0)
    terms_ref[FACETS] = jnp.zeros((256, TERMS), BF16)
    push_ref[FACETS] = jnp.zeros((16, 128), BF16)


def contact(
    terms_ref, push_ref, given_ref, force_ref, load_ref,
    table, listed, point_keep, points, force_sum, load_sum,
    sem, *buffers,
):
    gaps = [buffers[0:GROUP], buffers[GROUP : 2 * GROUP]]
    weights = [buffers[2 * GROUP : 3 * GROUP], buffers[3 * GROUP : 4 * GROUP]]
    copy = pltpu.make_async_copy(given_ref.at[:, pl.ds(48, 8), :], table, sem)
    copy.start()
    point_keep[...] = jnp.zeros(point_keep.shape, F32)
    force_sum[...] = jnp.zeros(force_sum.shape, F32)
    load_sum[...] = jnp.zeros(load_sum.shape, F32)
    points[PARTICLES] = jnp.zeros((TERMS, 256), BF16)

    def source(index, carry):
        for half in range(2):
            lanes = slice(128 * half, 128 * half + 128)
            place = [
                given_ref[index, 24 * half + 8 * part : 24 * half + 8 * part + 8, :]
                for part in range(3)
            ]
            square = place[0] * place[0] + place[1] * place[1] + place[2] * place[2]
            split = [split3(value) for value in place]
            for group, level in enumerate((0, 0, 0, 1, 1, 2)):
                for part in range(3):
                    point_keep[3 * group + part, :, lanes] = split[part][level]
            for level, value in enumerate(split3(-square)):
                point_keep[18 + level, :, lanes] = jnp.full((8, 128), 1.0, F32)
                point_keep[21 + level, :, lanes] = value
        for block in range(BLOCKS):
            points[index * BLOCKS + block] = point_keep[:, block, :].astype(BF16)
        return carry

    lax.fori_loop(0, DEPTH, source, 0)
    copy.wait()

    def gather(index, start):
        count = table[index, 0, 127].astype(jnp.int32)
        shift = index * (BLOCKS * 256)

        def entry(place, carry):
            listed[start + place] = table[index, 0, place].astype(jnp.int32) + shift
            return carry

        lax.fori_loop(0, count, entry, 0)
        return start + count

    total = lax.fori_loop(0, DEPTH, gather, 2 * GROUP)
    for spare in range(2 * GROUP):
        listed[spare] = PARTICLES * 256 + FACETS
    for spare in range(4 * GROUP):
        listed[total + spare] = PARTICLES * 256 + FACETS

    def exponents(place, buffer):
        code = listed[place]
        buffer[...] = jnp.dot(
            terms_ref[code & 255], points[code >> 8], preferred_element_type=F32
        )

    def weigh(buffer, weight_ref):
        for first in range(0, 128, 16):
            gap = buffer[first : first + 16, :]
            soft = jnp.where(gap > 80.0, gap, jnp.log(1.0 + jnp.exp(gap)))
            weight = jnp.exp(buffer[128 + first : 144 + first, :]) * soft
            high = weight.astype(BF16)
            weight_ref[first : first + 16, :] = high
            weight_ref[128 + first : 144 + first, :] = (weight - high.astype(F32)).astype(BF16)

    def add(place, weight_ref):
        code = listed[place]
        facet = code & 255
        push = push_ref[facet]
        result = jnp.dot(
            jnp.concatenate([push, push], axis=1), weight_ref[...], preferred_element_type=F32
        )
        result = result[0:8] + result[8:16]
        force_sum[code >> 8] += result
        load_sum[facet >> 2] += result[:, :128] + result[:, 128:]

    def step(index, carry):
        place = 2 * GROUP * index
        for half in range(2):
            here = place + half * GROUP
            for member in range(GROUP):
                exponents(here + 2 * GROUP + member, gaps[half][member])
                weigh(gaps[1 - half][member], weights[1 - half][member])
                add(here + member, weights[half][member])
        return carry

    lax.fori_loop(0, (total + 2 * GROUP - 1) // (2 * GROUP), step, 0)
    for index in range(DEPTH):
        for block in range(BLOCKS):
            for part in range(3):
                force_ref[index, 8 * part + block : 8 * part + block + 1, :] = force_sum[
                    index * BLOCKS + block, part : part + 1, :
                ]
    load_ref[...] = load_sum[0 : 2 * PLANE]


def finish_particles(force_ref, velocity_ref, mass_ref, out_ref):
    total = force_ref[0]
    for index in range(1, DEPTH):
        total = total + force_ref[index]
    scaled = TIME_STEP * mass_ref[...]
    for part in range(3):
        out_ref[part] = velocity_ref[part] + scaled * total[8 * part : 8 * part + 8, :]


def sum_loads(load_ref, out_ref):
    total = load_ref[0]
    for index in range(1, PLANE):
        total = total + load_ref[index]
    out_ref[...] = total


def finish_boulders(own_ref, other_ref, pose_ref, velocity_ref, out_ref):
    row = lax.broadcasted_iota(jnp.int32, (2, 6), 0)
    column = lax.broadcasted_iota(jnp.int32, (2, 6), 1)
    change = jnp.zeros((2, 6), F32)
    for boulder in range(2):
        total = jnp.sum(own_ref[boulder] + other_ref[boulder], axis=1, keepdims=True)
        force = [-total[part : part + 1, :] for part in range(3)]
        torque = [-total[3 + part : 4 + part, :] for part in range(3)]
        moves = [pose_ref[boulder, 12] * value for value in force]
        body = []
        for part in range(3):
            turned = (
                pose_ref[boulder, 3 + part] * torque[0]
                + pose_ref[boulder, 6 + part] * torque[1]
                + pose_ref[boulder, 9 + part] * torque[2]
            )
            body.append(turned * pose_ref[boulder, 13 + part])
        for part in range(3):
            moves.append(
                pose_ref[boulder, 3 + 3 * part] * body[0]
                + pose_ref[boulder, 4 + 3 * part] * body[1]
                + pose_ref[boulder, 5 + 3 * part] * body[2]
            )
        for part in range(6):
            here = jnp.logical_and(row == boulder, column == part)
            change = change + jnp.where(here, moves[part], 0.0)
    out_ref[...] = velocity_ref[...] + TIME_STEP * change


VMEM = pl.BlockSpec(memory_space=pltpu.VMEM)
SMEM = pl.BlockSpec(memory_space=pltpu.SMEM)


def call(kernel, outs, in_specs, scratch=(), cost=None):
    single = not isinstance(outs, list)
    return pl.pallas_call(
        kernel,
        out_shape=outs,
        in_specs=in_specs,
        out_specs=VMEM if single else [VMEM] * len(outs),
        scratch_shapes=list(scratch),
        cost_estimate=cost,
        compiler_params=pltpu.CompilerParams(vmem_limit_bytes=VMEM_LIMIT),
    )


def shards(
    particle_position,
    particle_velocity,
    inverse_mass,
    facet_geometry,
    boulder_pose,
    boulder_velocity,
    boulder_slot,
    block_home,
    pair_facet,
    pair_block,
    pair_active,
):
    owners = lax.axis_size("wide")
    planes = [[PLANE * depth + spot for spot in range(PLANE)] for depth in range(owners // PLANE)]
    columns = [[PLANE * depth + spot for depth in range(DEPTH)] for spot in range(PLANE)]
    swap = functools.partial(
        lax.all_to_all, axis_name="wide", split_axis=0, concat_axis=0, tiled=True
    )
    pairs = pair_facet.shape[0]
    shape = jax.ShapeDtypeStruct

    facets = call(facet_message, shape((PLANE, 8, BLOCKS, 128), F32), [VMEM, SMEM])(
        facet_geometry, boulder_pose
    )
    facets = swap(facets, axis_index_groups=planes)
    particles = call(pair_message, shape((DEPTH, 56, 128), F32), [VMEM] * 6)(
        particle_position.transpose(1, 0, 2),
        boulder_slot.reshape(2, 128),
        block_home.reshape(16, 128),
        pair_facet.reshape(pairs, 1),
        pair_block.reshape(pairs, 1),
        pair_active.reshape(pairs, 1),
    )
    particles = swap(particles, axis_index_groups=columns)
    terms, push = call(
        facet_features,
        [shape((FACETS + 1, 256, TERMS), BF16), shape((FACETS + 1, 16, 128), BF16)],
        [VMEM],
        [pltpu.VMEM((2 * TERMS, BLOCKS, 128), F32), pltpu.VMEM((16, BLOCKS, 128), F32)],
    )(facets)
    force, load = call(
        contact,
        [shape((DEPTH, 24, 256), F32), shape((2 * PLANE, 8, 128), F32)],
        [VMEM] * 3,
        [
            pltpu.SMEM((DEPTH, 8, 128), F32),
            pltpu.SMEM((DEPTH * 48 + 6 * GROUP,), jnp.int32),
            pltpu.VMEM((TERMS, BLOCKS, 256), F32),
            pltpu.VMEM((PARTICLES + 1, TERMS, 256), BF16),
            pltpu.VMEM((PARTICLES + 1, 8, 256), F32),
            pltpu.VMEM((2 * PLANE + 1, 8, 128), F32),
            pltpu.SemaphoreType.DMA,
        ]
        + [pltpu.VMEM((256, 256), F32)] * (2 * GROUP)
        + [pltpu.VMEM((256, 256), BF16)] * (2 * GROUP),
    )(terms, push, particles)
    load = swap(load, axis_index_groups=planes)
    load = call(sum_loads, shape((2, 8, 128), F32), [VMEM])(load.reshape(PLANE, 2, 8, 128))
    other = lax.ppermute(load, "narrow", [(0, 1), (1, 0)])
    boulder_motion = call(
        finish_boulders, shape(boulder_velocity.shape, F32), [VMEM, VMEM, SMEM, VMEM]
    )(load, other, boulder_pose, boulder_velocity)
    force = swap(force, axis_index_groups=columns)
    velocity = particle_velocity.transpose(1, 0, 2)
    new_velocity = call(finish_particles, shape(velocity.shape, F32), [VMEM] * 3)(
        force, velocity, inverse_mass
    )
    return (new_velocity.transpose(1, 0, 2), boulder_motion)


def solution(mesh):
    return jax.shard_map(
        shards,
        mesh=mesh,
        in_specs=(
            P(("wide", "narrow"), None, None),
            P(("wide", "narrow"), None, None),
            P(("wide", "narrow"), None),
            P("wide", None, None, None),
            P("wide", None),
            P("wide", None),
            P(),
            P(),
            P(("wide", "narrow")),
            P(("wide", "narrow")),
            P(("wide", "narrow")),
        ),
        out_specs=(P(("wide", "narrow"), None, None), P("wide", None)),
        check_vma=False,
    )
```

```python
import functools

import jax
import jax.numpy as jnp
from jax import lax
from jax.experimental import pallas as pl
from jax.experimental.pallas import tpu as pltpu
from jax.sharding import PartitionSpec as P

PENALTY = 0.3
SHARPNESS = 4.0
CONTACT_GAP = 0.1
TIME_STEP = 0.5

PLANE = 16
DEPTH = 8
BLOCKS = 8
TERMS = 32
FACETS = PLANE * BLOCKS
PARTICLES = DEPTH * BLOCKS
GROUP = 2
VMEM_LIMIT = 48 * 1024 * 1024

F32 = jnp.float32
BF16 = jnp.bfloat16


def split3(value):
    high = value.astype(BF16).astype(F32)
    rest = value - high
    middle = rest.astype(BF16).astype(F32)
    return high, middle, (rest - middle).astype(BF16).astype(F32)


def facet_message(geometry_ref, pose_ref, out_ref):
    lane = lax.broadcasted_iota(jnp.int32, (4, 128), 1)
    for boulder in range(2):
        part = [geometry_ref[boulder, row] for row in range(7)]
        center = [pose_ref[boulder, row] for row in range(3)]
        rotation = [pose_ref[boulder, 3 + entry] for entry in range(9)]
        rows = []
        for first in (0, 3):
            for row in range(3):
                rows.append(
                    rotation[3 * row] * part[first]
                    + rotation[3 * row + 1] * part[first + 1]
                    + rotation[3 * row + 2] * part[first + 2]
                )
        rows.append(part[6])
        rows.append(
            jnp.where(
                lane == 0,
                center[0],
                jnp.where(lane == 1, center[1], jnp.where(lane == 2, center[2], 0.0)),
            )
        )
        for target in range(PLANE):
            for row in range(8):
                out_ref[target, row, 4 * boulder : 4 * boulder + 4, :] = rows[row]


def pair_message(
    position_ref, slot_ref, home_ref, facet_ref, block_ref, active_ref, out_ref
):
    pairs = facet_ref.shape[0]
    lane = lax.broadcasted_iota(jnp.int32, (pairs, 128), 1)

    def look_up(table, index):
        rows = table.shape[0]
        row = lax.broadcasted_iota(jnp.int32, (pairs, rows), 1)
        onehot = ((index >> 7) == row).astype(F32).astype(BF16)
        picked = jnp.dot(onehot, table.astype(F32).astype(BF16), preferred_element_type=F32)
        picked = jnp.where(lane == (index & 127), picked, 0.0)
        return jnp.sum(picked, axis=1, keepdims=True).astype(jnp.int32)

    facet = facet_ref[...]
    slot = look_up(slot_ref[...], facet >> 2)
    local_block = look_up(home_ref[...] & 7, block_ref[...])
    plane = slot >> 5
    code = local_block * 256 + ((slot & 31) * 4 + (facet & 3))
    code = code.astype(F32)
    active = active_ref[...] != 0
    member = jnp.logical_and(lane == plane, active).astype(F32)
    row = lax.broadcasted_iota(jnp.int32, (pairs, pairs), 0)
    column = lax.broadcasted_iota(jnp.int32, (pairs, pairs), 1)
    below = (column < row).astype(F32).astype(BF16)
    before = jnp.dot(below, member.astype(BF16), preferred_element_type=F32)
    rank = jnp.sum(before * member, axis=1, keepdims=True).astype(jnp.int32)
    rank = jnp.where(active, rank, 255)
    spread = jnp.where(lane == rank, code, 0.0)
    lane_row = lax.broadcasted_iota(jnp.int32, (1, 128), 1)
    for target in range(DEPTH):
        here = jnp.logical_and(plane == target, active)
        listed = jnp.sum(jnp.where(here, spread, 0.0), axis=0, keepdims=True)
        count = jnp.sum(here.astype(F32), axis=0, keepdims=True)
        listed = jnp.where(lane_row == 127, count, listed)
        for half in range(2):
            for part in range(3):
                first = 24 * half + 8 * part
                out_ref[target, first : first + 8, :] = position_ref[
                    part, :, 128 * half : 128 * half + 128
                ]
        out_ref[target, 48:56, :] = jnp.broadcast_to(listed, (8, 128))


def facet_features(world_ref, out_ref, push_ref, terms_ref, terms_keep, push_keep, sem):
    terms_keep[...] = jnp.zeros(terms_keep.shape, F32)
    push_keep[...] = jnp.zeros(push_keep.shape, F32)

    def owner(index, carry):
        lever = [world_ref[index, part] for part in range(3)]
        normal = [world_ref[index, 3 + part] for part in range(3)]
        area = world_ref[index, 6]
        last = world_ref[index, 7]
        center = [lever[part] + last[:, part : part + 1] for part in range(3)]
        along = normal[0] * center[0] + normal[1] * center[1] + normal[2] * center[2]
        square = center[0] * center[0] + center[1] * center[1] + center[2] * center[2]
        sides = (
            ([-SHARPNESS * value for value in normal], SHARPNESS * (CONTACT_GAP + along), 0.0),
            ([2.0 * value for value in center], -square, 1.0),
        )
        for side, (factors, constant, tail) in enumerate(sides):
            split = [split3(value) for value in factors]
            order = (0, 1, 2, 0, 1, 0)
            for group, level in enumerate(order):
                for part in range(3):
                    terms_keep[side * TERMS + 3 * group + part] = split[part][level]
            for level, value in enumerate(split3(constant)):
                terms_keep[side * TERMS + 18 + level] = value
                terms_keep[side * TERMS + 21 + level] = jnp.full((8, 128), tail, F32)
        scaled = (PENALTY / SHARPNESS) * area
        push = [scaled * value for value in normal]
        push.append(lever[1] * push[2] - lever[2] * push[1])
        push.append(lever[2] * push[0] - lever[0] * push[2])
        push.append(lever[0] * push[1] - lever[1] * push[0])
        for part in range(6):
            high = push[part].astype(BF16).astype(F32)
            push_keep[part] = high
            push_keep[8 + part] = push[part] - high
        for block in range(BLOCKS):
            both = terms_keep[:, block, :]
            terms_ref[index * BLOCKS + block, 0:128, :] = both[:TERMS].T.astype(BF16)
            terms_ref[index * BLOCKS + block, 128:256, :] = both[TERMS:].T.astype(BF16)
            push_ref[index * BLOCKS + block] = push_keep[:, block, :].astype(BF16)
        part = pl.ds(index * BLOCKS, BLOCKS)
        pltpu.make_async_copy(terms_ref.at[part], out_ref.at[part], sem).start()
        return carry

    lax.fori_loop(0, PLANE, owner, 0)
    push_ref[FACETS] = jnp.zeros((16, 128), BF16)
    pltpu.make_async_copy(terms_ref, out_ref, sem).wait()


def contact(
    held_ref, push_ref, given_ref, force_ref, load_ref,
    terms_ref, terms_sem, table, listed, point_keep, points, force_sum, load_sum,
    sem, *buffers,
):
    gaps = [buffers[0:GROUP], buffers[GROUP : 2 * GROUP]]
    weights = [buffers[2 * GROUP : 3 * GROUP], buffers[3 * GROUP : 4 * GROUP]]
    copy = pltpu.make_async_copy(given_ref.at[:, pl.ds(48, 8), :], table, sem)
    copy.start()
    terms = pltpu.make_async_copy(held_ref, terms_ref.at[pl.ds(0, FACETS)], terms_sem)
    terms.start()
    terms_ref[FACETS] = jnp.zeros((256, TERMS), BF16)
    point_keep[...] = jnp.zeros(point_keep.shape, F32)
    force_sum[...] = jnp.zeros(force_sum.shape, F32)
    load_sum[...] = jnp.zeros(load_sum.shape, F32)
    points[PARTICLES] = jnp.zeros((TERMS, 256), BF16)

    def source(index, carry):
        for half in range(2):
            lanes = slice(128 * half, 128 * half + 128)
            place = [
                given_ref[index, 24 * half + 8 * part : 24 * half + 8 * part + 8, :]
                for part in range(3)
            ]
            square = place[0] * place[0] + place[1] * place[1] + place[2] * place[2]
            split = [split3(value) for value in place]
            for group, level in enumerate((0, 0, 0, 1, 1, 2)):
                for part in range(3):
                    point_keep[3 * group + part, :, lanes] = split[part][level]
            for level, value in enumerate(split3(-square)):
                point_keep[18 + level, :, lanes] = jnp.full((8, 128), 1.0, F32)
                point_keep[21 + level, :, lanes] = value
        for block in range(BLOCKS):
            points[index * BLOCKS + block] = point_keep[:, block, :].astype(BF16)
        return carry

    lax.fori_loop(0, DEPTH, source, 0)
    copy.wait()

    def gather(index, start):
        count = table[index, 0, 127].astype(jnp.int32)
        shift = index * (BLOCKS * 256)

        def entry(place, carry):
            listed[start + place] = table[index, 0, place].astype(jnp.int32) + shift
            return carry

        lax.fori_loop(0, count, entry, 0)
        return start + count

    total = lax.fori_loop(0, DEPTH, gather, 2 * GROUP)
    for spare in range(2 * GROUP):
        listed[spare] = PARTICLES * 256 + FACETS
    for spare in range(4 * GROUP):
        listed[total + spare] = PARTICLES * 256 + FACETS

    def exponents(place, buffer):
        code = listed[place]
        buffer[...] = jnp.dot(
            terms_ref[code & 255], points[code >> 8], preferred_element_type=F32
        )

    def weigh(buffer, weight_ref):
        for first in range(0, 128, 16):
            gap = buffer[first : first + 16, :]
            soft = jnp.where(gap > 80.0, gap, jnp.log(1.0 + jnp.exp(gap)))
            weight = jnp.exp(buffer[128 + first : 144 + first, :]) * soft
            high = weight.astype(BF16)
            weight_ref[first : first + 16, :] = high
            weight_ref[128 + first : 144 + first, :] = (weight - high.astype(F32)).astype(BF16)

    def add(place, weight_ref):
        code = listed[place]
        facet = code & 255
        push = push_ref[facet]
        result = jnp.dot(
            jnp.concatenate([push, push], axis=1), weight_ref[...], preferred_element_type=F32
        )
        result = result[0:8] + result[8:16]
        force_sum[code >> 8] += result
        load_sum[facet >> 2] += result[:, :128] + result[:, 128:]

    def step(index, carry):
        place = 2 * GROUP * index
        for half in range(2):
            here = place + half * GROUP
            for member in range(GROUP):
                exponents(here + 2 * GROUP + member, gaps[half][member])
                weigh(gaps[1 - half][member], weights[1 - half][member])
                add(here + member, weights[half][member])
        return carry

    terms.wait()
    lax.fori_loop(0, (total + 2 * GROUP - 1) // (2 * GROUP), step, 0)
    for index in range(DEPTH):
        for block in range(BLOCKS):
            for part in range(3):
                force_ref[index, 8 * part + block : 8 * part + block + 1, :] = force_sum[
                    index * BLOCKS + block, part : part + 1, :
                ]
    load_ref[...] = load_sum[0 : 2 * PLANE]


def finish_particles(force_ref, velocity_ref, mass_ref, out_ref):
    total = force_ref[0]
    for index in range(1, DEPTH):
        total = total + force_ref[index]
    scaled = TIME_STEP * mass_ref[...]
    for part in range(3):
        out_ref[part] = velocity_ref[part] + scaled * total[8 * part : 8 * part + 8, :]


def sum_loads(load_ref, out_ref):
    total = load_ref[0]
    for index in range(1, PLANE):
        total = total + load_ref[index]
    out_ref[...] = total


def finish_boulders(own_ref, other_ref, pose_ref, velocity_ref, out_ref):
    row = lax.broadcasted_iota(jnp.int32, (2, 6), 0)
    column = lax.broadcasted_iota(jnp.int32, (2, 6), 1)
    change = jnp.zeros((2, 6), F32)
    for boulder in range(2):
        total = jnp.sum(own_ref[boulder] + other_ref[boulder], axis=1, keepdims=True)
        force = [-total[part : part + 1, :] for part in range(3)]
        torque = [-total[3 + part : 4 + part, :] for part in range(3)]
        moves = [pose_ref[boulder, 12] * value for value in force]
        body = []
        for part in range(3):
            turned = (
                pose_ref[boulder, 3 + part] * torque[0]
                + pose_ref[boulder, 6 + part] * torque[1]
                + pose_ref[boulder, 9 + part] * torque[2]
            )
            body.append(turned * pose_ref[boulder, 13 + part])
        for part in range(3):
            moves.append(
                pose_ref[boulder, 3 + 3 * part] * body[0]
                + pose_ref[boulder, 4 + 3 * part] * body[1]
                + pose_ref[boulder, 5 + 3 * part] * body[2]
            )
        for part in range(6):
            here = jnp.logical_and(row == boulder, column == part)
            change = change + jnp.where(here, moves[part], 0.0)
    out_ref[...] = velocity_ref[...] + TIME_STEP * change


VMEM = pl.BlockSpec(memory_space=pltpu.VMEM)
SMEM = pl.BlockSpec(memory_space=pltpu.SMEM)
ANY = pl.BlockSpec(memory_space=pl.ANY)


def call(kernel, outs, in_specs, scratch=(), out_specs=VMEM):
    return pl.pallas_call(
        kernel,
        out_shape=outs,
        in_specs=in_specs,
        out_specs=out_specs,
        scratch_shapes=list(scratch),
        compiler_params=pltpu.CompilerParams(vmem_limit_bytes=VMEM_LIMIT),
    )


def shards(
    particle_position,
    particle_velocity,
    inverse_mass,
    facet_geometry,
    boulder_pose,
    boulder_velocity,
    boulder_slot,
    block_home,
    pair_facet,
    pair_block,
    pair_active,
):
    owners = lax.axis_size("wide")
    planes = [[PLANE * depth + spot for spot in range(PLANE)] for depth in range(owners // PLANE)]
    columns = [[PLANE * depth + spot for depth in range(DEPTH)] for spot in range(PLANE)]
    swap = functools.partial(
        lax.all_to_all, axis_name="wide", split_axis=0, concat_axis=0, tiled=True
    )
    pairs = pair_facet.shape[0]
    shape = jax.ShapeDtypeStruct

    facets = call(facet_message, shape((PLANE, 8, BLOCKS, 128), F32), [VMEM, SMEM])(
        facet_geometry.transpose(0, 2, 1, 3), boulder_pose
    )
    facets = swap(facets, axis_index_groups=planes)
    particles = call(pair_message, shape((DEPTH, 56, 128), F32), [VMEM] * 6)(
        particle_position.transpose(1, 0, 2),
        boulder_slot.reshape(2, 128),
        block_home.reshape(16, 128),
        pair_facet.reshape(pairs, 1),
        pair_block.reshape(pairs, 1),
        pair_active.reshape(pairs, 1),
    )
    particles = swap(particles, axis_index_groups=columns)
    terms, push = call(
        facet_features,
        [shape((FACETS, 256, TERMS), BF16), shape((FACETS + 1, 16, 128), BF16)],
        [VMEM],
        [
            pltpu.VMEM((FACETS, 256, TERMS), BF16),
            pltpu.VMEM((2 * TERMS, BLOCKS, 128), F32),
            pltpu.VMEM((16, BLOCKS, 128), F32),
            pltpu.SemaphoreType.DMA,
        ],
        out_specs=[ANY, VMEM],
    )(facets)
    force, load = call(
        contact,
        [shape((DEPTH, 24, 256), F32), shape((2 * PLANE, 8, 128), F32)],
        [ANY, VMEM, VMEM],
        [
            pltpu.VMEM((FACETS + 1, 256, TERMS), BF16),
            pltpu.SemaphoreType.DMA,
            pltpu.SMEM((DEPTH, 8, 128), F32),
            pltpu.SMEM((DEPTH * 48 + 6 * GROUP,), jnp.int32),
            pltpu.VMEM((TERMS, BLOCKS, 256), F32),
            pltpu.VMEM((PARTICLES + 1, TERMS, 256), BF16),
            pltpu.VMEM((PARTICLES + 1, 8, 256), F32),
            pltpu.VMEM((2 * PLANE + 1, 8, 128), F32),
            pltpu.SemaphoreType.DMA,
        ]
        + [pltpu.VMEM((256, 256), F32)] * (2 * GROUP)
        + [pltpu.VMEM((256, 256), BF16)] * (2 * GROUP),
        out_specs=[VMEM, VMEM],
    )(terms, push, particles)
    grid = load.reshape(4, 4, 2, 8, 128)
    spot = lax.axis_index("wide") % PLANE
    down, across = spot // 4, spot % 4

    def shift(step, unit):
        moves = []
        for device in range(owners):
            place = device // unit % 4
            moves.append((device, device + ((place + step) % 4 - place) * unit))
        return moves

    def pick(array, axis, index):
        return lax.dynamic_index_in_dim(array, index % 4, axis, keepdims=False)

    row = pick(grid, 1, across)
    for step in (1, 2, 3):
        row = row + lax.ppermute(pick(grid, 1, across + step), "wide", shift(step, 1))
    load = pick(row, 0, down)
    for step in (1, 2, 3):
        load = load + lax.ppermute(pick(row, 0, down + step), "wide", shift(step, 4))
    other = lax.ppermute(load, "narrow", [(0, 1), (1, 0)])
    boulder_motion = call(
        finish_boulders, shape(boulder_velocity.shape, F32), [VMEM, VMEM, SMEM, VMEM]
    )(load, other, boulder_pose, boulder_velocity)
    force = swap(force, axis_index_groups=columns)
    velocity = particle_velocity.transpose(1, 0, 2)
    new_velocity = call(finish_particles, shape(velocity.shape, F32), [VMEM] * 3)(
        force, velocity, inverse_mass
    )
    return (new_velocity.transpose(1, 0, 2), boulder_motion)


def solution(mesh):
    return jax.shard_map(
        shards,
        mesh=mesh,
        in_specs=(
            P(("wide", "narrow"), None, None),
            P(("wide", "narrow"), None, None),
            P(("wide", "narrow"), None),
            P("wide", None, None, None),
            P("wide", None),
            P("wide", None),
            P(),
            P(),
            P(("wide", "narrow")),
            P(("wide", "narrow")),
            P(("wide", "narrow")),
        ),
        out_specs=(P(("wide", "narrow"), None, None), P("wide", None)),
        check_vma=False,
    )
```

```python
import functools

import jax
import jax.numpy as jnp
from jax import lax
from jax.experimental import pallas as pl
from jax.experimental.pallas import tpu as pltpu
from jax.sharding import PartitionSpec as P

PENALTY = 0.3
SHARPNESS = 4.0
CONTACT_GAP = 0.1
TIME_STEP = 0.5

PLANE = 16
DEPTH = 8
BLOCKS = 8
TERMS = 32
PITCH = 9
FACETS = PLANE * BLOCKS
ROW = 4 * BLOCKS
PARTICLES = DEPTH * BLOCKS
GROUP = 2
VMEM_LIMIT = 48 * 1024 * 1024
WHOLE_VMEM = 63 * 1024 * 1024

F32 = jnp.float32
BF16 = jnp.bfloat16


def split3(value):
    high = value.astype(BF16).astype(F32)
    rest = value - high
    middle = rest.astype(BF16).astype(F32)
    return high, middle, (rest - middle).astype(BF16).astype(F32)


def put(keep, row, value):
    keep[PITCH * row : PITCH * row + BLOCKS, :] = value


def fetch(pairs, sems):
    copies = [
        pltpu.make_async_copy(origin, target, sems.at[index])
        for index, (origin, target) in enumerate(pairs)
    ]
    for copy in copies:
        copy.start()
    for copy in copies:
        copy.wait()


def facet_message(geometry_at, pose_at, out_ref, geometry_ref, pose_ref, sems):
    fetch([(geometry_at, geometry_ref), (pose_at, pose_ref)], sems)
    lane = lax.broadcasted_iota(jnp.int32, (4, 128), 1)
    for boulder in range(2):
        part = [geometry_ref[boulder, row] for row in range(7)]
        center = [pose_ref[boulder, row] for row in range(3)]
        rotation = [pose_ref[boulder, 3 + entry] for entry in range(9)]
        rows = []
        for first in (0, 3):
            for row in range(3):
                rows.append(
                    rotation[3 * row] * part[first]
                    + rotation[3 * row + 1] * part[first + 1]
                    + rotation[3 * row + 2] * part[first + 2]
                )
        rows.append(part[6])
        rows.append(
            jnp.where(
                lane == 0,
                center[0],
                jnp.where(lane == 1, center[1], jnp.where(lane == 2, center[2], 0.0)),
            )
        )
        for row in range(8):
            out_ref[row, 4 * boulder : 4 * boulder + 4, :] = rows[row]


def pair_message(*refs):
    held, out_ref, (position_ref, slot_ref, home_ref), rows, sems = (
        refs[:6], refs[7], refs[8:11], refs[11:14], refs[14],
    )
    fetch(list(zip(held, (position_ref, slot_ref, home_ref, *rows))), sems)
    facet, block, active = [row[...] for row in rows]
    pairs = facet.shape[1]
    packed = jnp.where(active != 0, 1, 0) + 2 * facet + 2048 * block
    packed = jnp.broadcast_to(packed, (128, pairs)).T[:, 0:1]
    active = (packed & 1) != 0
    facet = (packed >> 1) & 1023
    block = packed >> 11
    lane = lax.broadcasted_iota(jnp.int32, (pairs, 128), 1)

    def look_up(table, index):
        rows = table.shape[0]
        row = lax.broadcasted_iota(jnp.int32, (pairs, rows), 1)
        onehot = ((index >> 7) == row).astype(F32).astype(BF16)
        picked = jnp.dot(onehot, table.astype(F32).astype(BF16), preferred_element_type=F32)
        picked = jnp.where(lane == (index & 127), picked, 0.0)
        return jnp.sum(picked, axis=1, keepdims=True).astype(jnp.int32)

    slot = look_up(slot_ref[...], facet >> 2)
    local_block = look_up(home_ref[...] & 7, block)
    plane = slot >> 5
    code = local_block * 256 + ((slot & 31) * 4 + (facet & 3))
    code = code.astype(F32)
    late = ((lax.axis_index("wide") >> 2) - (slot >> 3)) & 2
    member = jnp.logical_and(lane == plane + DEPTH * (late >> 1), active).astype(F32)
    row = lax.broadcasted_iota(jnp.int32, (pairs, pairs), 0)
    column = lax.broadcasted_iota(jnp.int32, (pairs, pairs), 1)
    below = (column < row).astype(F32).astype(BF16)
    before = jnp.dot(below, member.astype(BF16), preferred_element_type=F32)
    rank = jnp.sum(before * member, axis=1, keepdims=True)
    early = jnp.sum(member, axis=0, keepdims=True)
    ahead = jnp.where(jnp.logical_and(lane == plane, late > 0), early, 0.0)
    rank = (rank + jnp.sum(ahead, axis=1, keepdims=True)).astype(jnp.int32)
    rank = jnp.where(active, rank, 255)
    spread = jnp.where(lane == rank, code, 0.0)
    lane_row = lax.broadcasted_iota(jnp.int32, (1, 128), 1)
    for target in range(DEPTH):
        here = jnp.logical_and(plane == target, active)
        listed = jnp.sum(jnp.where(here, spread, 0.0), axis=0, keepdims=True)
        count = jnp.sum(here.astype(F32), axis=0, keepdims=True)
        first = jnp.sum(jnp.where(lane_row == target, early, 0.0), axis=1, keepdims=True)
        listed = jnp.where(lane_row == 126, first, jnp.where(lane_row == 127, count, listed))
        for half in range(2):
            for part in range(3):
                first = 24 * half + 8 * part
                out_ref[target, first : first + 8, :] = position_ref[
                    part, :, 128 * half : 128 * half + 128
                ]
        out_ref[target, 48:56, :] = jnp.broadcast_to(listed, (8, 128))


def facet_features(*refs):
    *world_refs, out_ref, push_ref, terms_ref, terms_keep, push_keep, sem = refs
    across = lax.axis_index("wide") & 3
    terms_keep[...] = jnp.zeros(terms_keep.shape, F32)
    push_keep[...] = jnp.zeros(push_keep.shape, F32)

    def owner(number, world_ref, step):
        index = 4 * number + ((across - step) & 3)
        lever = [world_ref[step, part] for part in range(3)]
        normal = [world_ref[step, 3 + part] for part in range(3)]
        area = world_ref[step, 6]
        last = world_ref[step, 7]
        center = [lever[part] + last[:, part : part + 1] for part in range(3)]
        along = normal[0] * center[0] + normal[1] * center[1] + normal[2] * center[2]
        square = center[0] * center[0] + center[1] * center[1] + center[2] * center[2]
        sides = (
            ([-SHARPNESS * value for value in normal], SHARPNESS * (CONTACT_GAP + along), 0.0),
            ([2.0 * value for value in center], -square, 1.0),
        )
        for side, (factors, constant, tail) in enumerate(sides):
            split = [split3(value) for value in factors]
            order = (0, 1, 2, 0, 1, 0)
            for group, level in enumerate(order):
                for part in range(3):
                    put(terms_keep, side * TERMS + 3 * group + part, split[part][level])
            for level, value in enumerate(split3(constant)):
                put(terms_keep, side * TERMS + 18 + level, value)
                put(terms_keep, side * TERMS + 21 + level, jnp.full((8, 128), tail, F32))
        scaled = (PENALTY / SHARPNESS) * area
        push = [scaled * value for value in normal]
        push.append(lever[1] * push[2] - lever[2] * push[1])
        push.append(lever[2] * push[0] - lever[0] * push[2])
        push.append(lever[0] * push[1] - lever[1] * push[0])
        for part in range(6):
            high = push[part].astype(BF16).astype(F32)
            put(push_keep, part, high)
            put(push_keep, 8 + part, push[part] - high)
        for block in range(BLOCKS):
            both = terms_keep[pl.ds(block, 2 * TERMS, stride=PITCH), :]
            terms_ref[index * BLOCKS + block, 0:128, :] = both[:TERMS].T.astype(BF16)
            terms_ref[index * BLOCKS + block, 128:256, :] = both[TERMS:].T.astype(BF16)
            push_ref[index * BLOCKS + block] = push_keep[
                pl.ds(block, 16, stride=PITCH), :
            ].astype(BF16)
        part = pl.ds(index * BLOCKS, BLOCKS)
        pltpu.make_async_copy(terms_ref.at[part], out_ref.at[part], sem).start()

    for number, world_ref in enumerate(world_refs):

        def step(index, carry):
            owner(number, world_ref, index)
            return carry

        lax.fori_loop(0, 4, step, 0)
    pltpu.make_async_copy(terms_ref, out_ref, sem).wait()


def contact(
    near_terms, far_terms, near_push, far_push, given_ref, force_ref, load_ref,
    terms_ref, push_ref, held_sem, table, listed, near_keep, far_keep, points, force_sum, load_sum,
    sem, *buffers,
):
    gaps = [buffers[0:GROUP], buffers[GROUP : 2 * GROUP]]
    weights = [buffers[2 * GROUP : 3 * GROUP], buffers[3 * GROUP : 4 * GROUP]]
    copy = pltpu.make_async_copy(given_ref.at[:, pl.ds(48, 8), :], table, sem)
    copy.start()
    down = lax.axis_index("wide") >> 2
    held = []
    for step in range(4):
        target = pl.ds(ROW * ((down - step) & 3), ROW)
        source_at = pl.ds(ROW * max(step - 1, 0), ROW)
        pairs = ((near_terms, far_terms, terms_ref), (near_push, far_push, push_ref))
        for kind, (near, far, whole) in enumerate(pairs):
            origin = far if step else near
            held.append(
                pltpu.make_async_copy(
                    origin.at[source_at], whole.at[target], held_sem.at[2 * step + kind]
                )
            )
            held[-1].start()
    terms_ref[FACETS] = jnp.zeros((256, TERMS), BF16)
    push_ref[FACETS] = jnp.zeros((16, 128), BF16)
    point_keep = [near_keep, far_keep]
    for keep in point_keep:
        keep[...] = jnp.zeros(keep.shape, F32)
    force_sum[...] = jnp.zeros(force_sum.shape, F32)
    load_sum[...] = jnp.zeros(load_sum.shape, F32)
    points[PARTICLES] = jnp.zeros((TERMS, 256), BF16)

    def source(index, carry):
        for half in range(2):
            keep = point_keep[half]
            place = [
                given_ref[index, 24 * half + 8 * part : 24 * half + 8 * part + 8, :]
                for part in range(3)
            ]
            square = place[0] * place[0] + place[1] * place[1] + place[2] * place[2]
            split = [split3(value) for value in place]
            for group, level in enumerate((0, 0, 0, 1, 1, 2)):
                for part in range(3):
                    put(keep, 3 * group + part, split[part][level])
            for level, value in enumerate(split3(-square)):
                put(keep, 18 + level, jnp.full((8, 128), 1.0, F32))
                put(keep, 21 + level, value)
        for block in range(BLOCKS):
            for half in range(2):
                points[index * BLOCKS + block, :, 128 * half : 128 * half + 128] = point_keep[half][
                    pl.ds(block, TERMS, stride=PITCH), :
                ].astype(BF16)
        return carry

    lax.fori_loop(0, DEPTH, source, 0)
    copy.wait()

    def gather(late, start):
        def one(index, start):
            early = table[index, 0, 126].astype(jnp.int32)
            first = jnp.where(late, early, 0)
            count = jnp.where(late, table[index, 0, 127].astype(jnp.int32) - early, early)
            shift = index * (BLOCKS * 256)

            def entry(place, carry):
                listed[start + place] = table[index, 0, first + place].astype(jnp.int32) + shift
                return carry

            lax.fori_loop(0, count, entry, 0)
            return start + count

        return lax.fori_loop(0, DEPTH, one, start)

    early = gather(False, 2 * GROUP)
    total = gather(True, early)
    for spare in range(2 * GROUP):
        listed[spare] = PARTICLES * 256 + FACETS
    for spare in range(4 * GROUP):
        listed[total + spare] = PARTICLES * 256 + FACETS

    def exponents(place, buffer):
        code = listed[place]
        buffer[...] = jnp.dot(
            terms_ref[code & 255], points[code >> 8], preferred_element_type=F32
        )

    def weigh(buffer, weight_ref):
        for first in range(0, 128, 16):
            gap = buffer[first : first + 16, :]
            soft = jnp.where(gap > 80.0, gap, jnp.log(1.0 + jnp.exp(gap)))
            weight = jnp.exp(buffer[128 + first : 144 + first, :]) * soft
            high = weight.astype(BF16)
            weight_ref[first : first + 16, :] = high
            weight_ref[128 + first : 144 + first, :] = (weight - high.astype(F32)).astype(BF16)

    def add(place, weight_ref):
        code = listed[place]
        facet = code & 255
        push = push_ref[facet]
        result = jnp.dot(
            jnp.concatenate([push, push], axis=1), weight_ref[...], preferred_element_type=F32
        )
        result = result[0:8] + result[8:16]
        force_sum[code >> 8] += result
        load_sum[facet >> 2] += result[:, :128] + result[:, 128:]

    def step(index, carry):
        place = 2 * GROUP * index
        for half in range(2):
            here = place + half * GROUP
            for member in range(GROUP):
                exponents(here + 2 * GROUP + member, gaps[half][member])
                weigh(gaps[1 - half][member], weights[1 - half][member])
                add(here + member, weights[half][member])
        return carry

    for one in held[:4]:
        one.wait()
    steps = (early - 2 * GROUP) // (2 * GROUP)
    lax.fori_loop(0, steps, step, 0)
    for one in held[4:]:
        one.wait()
    lax.fori_loop(steps, (total + 2 * GROUP - 1) // (2 * GROUP), step, 0)
    for index in range(DEPTH):
        for block in range(BLOCKS):
            for part in range(3):
                force_ref[index, 8 * part + block : 8 * part + block + 1, :] = force_sum[
                    index * BLOCKS + block, part : part + 1, :
                ]
    load_ref[...] = load_sum[0 : 2 * PLANE]


def finish(
    force_ref, velocity_ref, mass_ref, own_ref, other_ref, pose_at, motion_at, out_ref, motion_ref,
    pose_ref, spin_ref, sems,
):
    fetch([(pose_at, pose_ref), (motion_at, spin_ref)], sems)
    finish_boulders(own_ref, other_ref, pose_ref, spin_ref, motion_ref)
    total = force_ref[0]
    for index in range(1, DEPTH):
        total = total + force_ref[index]
    scaled = TIME_STEP * mass_ref[...]
    for part in range(3):
        out_ref[part] = velocity_ref[part] + scaled * total[8 * part : 8 * part + 8, :]


def finish_boulders(own_ref, other_ref, pose_ref, velocity_ref, out_ref):
    row = lax.broadcasted_iota(jnp.int32, (2, 6), 0)
    column = lax.broadcasted_iota(jnp.int32, (2, 6), 1)
    change = jnp.zeros((2, 6), F32)
    for boulder in range(2):
        total = jnp.sum(own_ref[boulder] + other_ref[boulder], axis=1, keepdims=True)
        force = [-total[part : part + 1, :] for part in range(3)]
        torque = [-total[3 + part : 4 + part, :] for part in range(3)]
        moves = [pose_ref[boulder, 12] * value for value in force]
        body = []
        for part in range(3):
            turned = (
                pose_ref[boulder, 3 + part] * torque[0]
                + pose_ref[boulder, 6 + part] * torque[1]
                + pose_ref[boulder, 9 + part] * torque[2]
            )
            body.append(turned * pose_ref[boulder, 13 + part])
        for part in range(3):
            moves.append(
                pose_ref[boulder, 3 + 3 * part] * body[0]
                + pose_ref[boulder, 4 + 3 * part] * body[1]
                + pose_ref[boulder, 5 + 3 * part] * body[2]
            )
        for part in range(6):
            here = jnp.logical_and(row == boulder, column == part)
            change = change + jnp.where(here, moves[part], 0.0)
    out_ref[...] = velocity_ref[...] + TIME_STEP * change


VMEM = pl.BlockSpec(memory_space=pltpu.VMEM)
ANY = pl.BlockSpec(memory_space=pl.ANY)


def call(kernel, outs, in_specs, scratch=(), out_specs=VMEM, limit=VMEM_LIMIT):
    return pl.pallas_call(
        kernel,
        out_shape=outs,
        in_specs=in_specs,
        out_specs=out_specs,
        scratch_shapes=list(scratch),
        compiler_params=pltpu.CompilerParams(vmem_limit_bytes=limit),
    )


def shards(
    particle_position,
    particle_velocity,
    inverse_mass,
    facet_geometry,
    boulder_pose,
    boulder_velocity,
    boulder_slot,
    block_home,
    pair_facet,
    pair_block,
    pair_active,
):
    owners = lax.axis_size("wide")
    columns = [[PLANE * depth + spot for depth in range(DEPTH)] for spot in range(PLANE)]
    swap = functools.partial(
        lax.all_to_all, axis_name="wide", split_axis=0, concat_axis=0, tiled=True
    )
    pairs = pair_facet.shape[0]
    shape = jax.ShapeDtypeStruct

    def shift(step, unit):
        moves = []
        for device in range(owners):
            place = device // unit % 4
            moves.append((device, device + ((place + step) % 4 - place) * unit))
        return moves

    geometry = facet_geometry.transpose(0, 2, 1, 3)
    own = call(
        facet_message,
        shape((8, BLOCKS, 128), F32),
        [ANY, ANY],
        [
            pltpu.VMEM(geometry.shape, F32),
            pltpu.SMEM(boulder_pose.shape, F32),
            pltpu.SemaphoreType.DMA((2,)),
        ],
        limit=WHOLE_VMEM,
    )(geometry, boulder_pose)
    line = [own] + [lax.ppermute(own, "wide", shift(step, 1)) for step in (1, 2, 3)]
    line = jnp.stack(line)
    lists = [
        particle_position.transpose(1, 0, 2),
        boulder_slot.reshape(-1, 128),
        block_home.reshape(-1, 128),
        pair_facet.reshape(1, pairs),
        pair_block.reshape(1, pairs),
        pair_active.reshape(1, pairs),
    ]
    particles = call(
        pair_message,
        shape((DEPTH, 56, 128), F32),
        [ANY] * 7,
        [pltpu.VMEM(value.shape, value.dtype) for value in lists]
        + [pltpu.SemaphoreType.DMA((6,))],
        limit=WHOLE_VMEM,
    )(*lists, own)
    lines = [lax.ppermute(line, "wide", shift(step, 4)) for step in (1, 2, 3)]

    def features(parts):
        blocks = ROW * len(parts)
        return call(
            facet_features,
            [shape((blocks, 256, TERMS), BF16), shape((blocks, 16, 128), BF16)],
            [VMEM] * len(parts),
            [
                pltpu.VMEM((blocks, 256, TERMS), BF16),
                pltpu.VMEM((2 * TERMS * PITCH, 128), F32),
                pltpu.VMEM((16 * PITCH, 128), F32),
                pltpu.SemaphoreType.DMA,
            ],
            out_specs=[ANY, VMEM],
        )(*parts)

    near_terms, near_push = features([line])
    particles, near_push = lax.optimization_barrier((particles, near_push))
    particles = swap(particles, axis_index_groups=columns)
    far_terms, far_push = features(lines)
    force, load = call(
        contact,
        [shape((DEPTH, 24, 256), F32), shape((2 * PLANE, 8, 128), F32)],
        [ANY] * 4 + [VMEM],
        [
            pltpu.VMEM((FACETS + 1, 256, TERMS), BF16),
            pltpu.VMEM((FACETS + 1, 16, 128), BF16),
            pltpu.SemaphoreType.DMA((8,)),
            pltpu.SMEM((DEPTH, 8, 128), F32),
            pltpu.SMEM((DEPTH * 48 + 6 * GROUP,), jnp.int32),
            pltpu.VMEM((TERMS * PITCH, 128), F32),
            pltpu.VMEM((TERMS * PITCH, 128), F32),
            pltpu.VMEM((PARTICLES + 1, TERMS, 256), BF16),
            pltpu.VMEM((PARTICLES + 1, 8, 256), F32),
            pltpu.VMEM((2 * PLANE + 1, 8, 128), F32),
            pltpu.SemaphoreType.DMA,
        ]
        + [pltpu.VMEM((256, 256), F32)] * (2 * GROUP)
        + [pltpu.VMEM((256, 256), BF16)] * (2 * GROUP),
        out_specs=[VMEM, VMEM],
    )(near_terms, far_terms, near_push, far_push, particles)
    grid = load.reshape(4, 4, 2, 8, 128)
    spot = lax.axis_index("wide") % PLANE
    down, across = spot // 4, spot % 4
    def pick(array, axis, index):
        return lax.dynamic_index_in_dim(array, index % 4, axis, keepdims=False)

    row = pick(grid, 1, across)
    for step in (1, 2, 3):
        row = row + lax.ppermute(pick(grid, 1, across + step), "wide", shift(step, 1))
    load = pick(row, 0, down)
    for step in (1, 2, 3):
        load = load + lax.ppermute(pick(row, 0, down + step), "wide", shift(step, 4))
    other = lax.ppermute(load, "narrow", [(0, 1), (1, 0)])
    force = swap(force, axis_index_groups=columns)
    velocity = particle_velocity.transpose(1, 0, 2)
    new_velocity, boulder_motion = call(
        finish,
        [shape(velocity.shape, F32), shape(boulder_velocity.shape, F32)],
        [VMEM] * 5 + [ANY] * 2,
        [
            pltpu.SMEM(boulder_pose.shape, F32),
            pltpu.VMEM(boulder_velocity.shape, F32),
            pltpu.SemaphoreType.DMA((2,)),
        ],
        out_specs=[VMEM, VMEM],
    )(force, velocity, inverse_mass, load, other, boulder_pose, boulder_velocity)
    return (new_velocity.transpose(1, 0, 2), boulder_motion)


def solution(mesh):
    return jax.shard_map(
        shards,
        mesh=mesh,
        in_specs=(
            P(("wide", "narrow"), None, None),
            P(("wide", "narrow"), None, None),
            P(("wide", "narrow"), None),
            P("wide", None, None, None),
            P("wide", None),
            P("wide", None),
            P(),
            P(),
            P(("wide", "narrow")),
            P(("wide", "narrow")),
            P(("wide", "narrow")),
        ),
        out_specs=(P(("wide", "narrow"), None, None), P("wide", None)),
        check_vma=False,
    )
```

```python
import functools

import jax
import jax.numpy as jnp
from jax import lax
from jax.experimental import pallas as pl
from jax.experimental.pallas import tpu as pltpu
from jax.sharding import PartitionSpec as P

PENALTY = 0.3
SHARPNESS = 4.0
CONTACT_GAP = 0.1
TIME_STEP = 0.5

PLANE = 16
DEPTH = 8
BLOCKS = 8
TERMS = 32
PITCH = 9
FACETS = PLANE * BLOCKS
ROW = 4 * BLOCKS
PARTICLES = DEPTH * BLOCKS
GROUP = 2
SIDE = 4
VMEM_LIMIT = 48 * 1024 * 1024
WHOLE_VMEM = 63 * 1024 * 1024

F32 = jnp.float32
BF16 = jnp.bfloat16


def split3(value):
    high = value.astype(BF16).astype(F32)
    rest = value - high
    middle = rest.astype(BF16).astype(F32)
    return high, middle, (rest - middle).astype(BF16).astype(F32)


def put(keep, row, value):
    keep[PITCH * row : PITCH * row + BLOCKS, :] = value


def fetch(pairs, sems):
    copies = [
        pltpu.make_async_copy(origin, target, sems.at[index])
        for index, (origin, target) in enumerate(pairs)
    ]
    for copy in copies:
        copy.start()
    for copy in copies:
        copy.wait()


def facet_message(geometry_at, pose_at, out_ref, geometry_ref, pose_ref, sems):
    fetch([(geometry_at, geometry_ref), (pose_at, pose_ref)], sems)
    lane = lax.broadcasted_iota(jnp.int32, (4, 128), 1)
    for boulder in range(2):
        part = [geometry_ref[boulder, row] for row in range(7)]
        center = [pose_ref[boulder, row] for row in range(3)]
        rotation = [pose_ref[boulder, 3 + entry] for entry in range(9)]
        rows = []
        for first in (0, 3):
            for row in range(3):
                rows.append(
                    rotation[3 * row] * part[first]
                    + rotation[3 * row + 1] * part[first + 1]
                    + rotation[3 * row + 2] * part[first + 2]
                )
        rows.append(part[6])
        rows.append(
            jnp.where(
                lane == 0,
                center[0],
                jnp.where(lane == 1, center[1], jnp.where(lane == 2, center[2], 0.0)),
            )
        )
        for target in range(PLANE):
            for row in range(8):
                out_ref[target, row, 4 * boulder : 4 * boulder + 4, :] = rows[row]


def pair_message(*refs):
    held, (out_ref, own_ref), (position_ref, slot_ref, home_ref), rows, sems = (
        refs[:6], refs[6:8], refs[8:11], refs[11:14], refs[14],
    )
    fetch(list(zip(held, (position_ref, slot_ref, home_ref, *rows))), sems)
    facet, block, active = [row[...] for row in rows]
    pairs = facet.shape[1]
    packed = jnp.where(active != 0, 1, 0) + 2 * facet + 2048 * block
    packed = jnp.broadcast_to(packed, (128, pairs)).T[:, 0:1]
    active = (packed & 1) != 0
    facet = (packed >> 1) & 1023
    block = packed >> 11
    lane = lax.broadcasted_iota(jnp.int32, (pairs, 128), 1)

    def look_up(table, index):
        rows = table.shape[0]
        row = lax.broadcasted_iota(jnp.int32, (pairs, rows), 1)
        onehot = ((index >> 7) == row).astype(F32).astype(BF16)
        picked = jnp.dot(onehot, table.astype(F32).astype(BF16), preferred_element_type=F32)
        picked = jnp.where(lane == (index & 127), picked, 0.0)
        return jnp.sum(picked, axis=1, keepdims=True).astype(jnp.int32)

    slot = look_up(slot_ref[...], facet >> 2)
    local_block = look_up(home_ref[...] & 7, block)
    plane = slot >> 5
    code = local_block * 256 + ((slot & 31) * 4 + (facet & 3))
    code = code.astype(F32)
    late = (slot >> 3) & 2
    member = jnp.logical_and(lane == plane + DEPTH * (late >> 1), active).astype(F32)
    row = lax.broadcasted_iota(jnp.int32, (pairs, pairs), 0)
    column = lax.broadcasted_iota(jnp.int32, (pairs, pairs), 1)
    below = (column < row).astype(F32).astype(BF16)
    before = jnp.dot(below, member.astype(BF16), preferred_element_type=F32)
    rank = jnp.sum(before * member, axis=1, keepdims=True)
    early = jnp.sum(member, axis=0, keepdims=True)
    ahead = jnp.where(jnp.logical_and(lane == plane, late > 0), early, 0.0)
    rank = (rank + jnp.sum(ahead, axis=1, keepdims=True)).astype(jnp.int32)
    rank = jnp.where(active, rank, 255)
    spread = jnp.where(lane == rank, code, 0.0)
    lane_row = lax.broadcasted_iota(jnp.int32, (1, 128), 1)
    for target in range(DEPTH):
        here = jnp.logical_and(plane == target, active)
        listed = jnp.sum(jnp.where(here, spread, 0.0), axis=0, keepdims=True)
        count = jnp.sum(here.astype(F32), axis=0, keepdims=True)
        first = jnp.sum(jnp.where(lane_row == target, early, 0.0), axis=1, keepdims=True)
        listed = jnp.where(lane_row == 126, first, jnp.where(lane_row == 127, count, listed))
        for half in range(2):
            for part in range(3):
                first = 24 * half + 8 * part
                out_ref[target, first : first + 8, :] = position_ref[
                    part, :, 128 * half : 128 * half + 128
                ]
        out_ref[target, 48:56, :] = jnp.broadcast_to(listed, (8, 128))
    own_ref[...] = out_ref[lax.axis_index("wide") // PLANE]


def particle_terms(place_ref, points, first, point_keep):
    for half in range(2):
        keep = point_keep[half]
        place = [
            place_ref[24 * half + 8 * part : 24 * half + 8 * part + 8, :]
            for part in range(3)
        ]
        square = place[0] * place[0] + place[1] * place[1] + place[2] * place[2]
        split = [split3(value) for value in place]
        for group, level in enumerate((0, 0, 0, 1, 1, 2)):
            for part in range(3):
                put(keep, 3 * group + part, split[part][level])
        for level, value in enumerate(split3(-square)):
            put(keep, 18 + level, jnp.full((8, 128), 1.0, F32))
            put(keep, 21 + level, value)
    for block in range(BLOCKS):
        for half in range(2):
            points[first + block, :, 128 * half : 128 * half + 128] = point_keep[half][
                pl.ds(block, TERMS, stride=PITCH), :
            ].astype(BF16)


def pipeline(terms_ref, push_ref, points, listed, force_sum, load_sum, buffers):
    gaps = [buffers[0:GROUP], buffers[GROUP : 2 * GROUP]]
    weights = [buffers[2 * GROUP : 3 * GROUP], buffers[3 * GROUP : 4 * GROUP]]

    def exponents(place, buffer):
        code = listed[place]
        buffer[...] = jnp.dot(
            terms_ref[code & 255], points[code >> 8], preferred_element_type=F32
        )

    def weigh(buffer, weight_ref):
        for first in range(0, 128, 16):
            gap = buffer[first : first + 16, :]
            soft = jnp.where(gap > 80.0, gap, jnp.log(1.0 + jnp.exp(gap)))
            weight = jnp.exp(buffer[128 + first : 144 + first, :]) * soft
            high = weight.astype(BF16)
            weight_ref[first : first + 16, :] = high
            weight_ref[128 + first : 144 + first, :] = (weight - high.astype(F32)).astype(BF16)

    def add(place, weight_ref):
        code = listed[place]
        facet = code & 255
        push = push_ref[facet]
        result = jnp.dot(
            jnp.concatenate([push, push], axis=1), weight_ref[...], preferred_element_type=F32
        )
        result = result[0:8] + result[8:16]
        force_sum[code >> 8] += result
        load_sum[facet >> 2] += result[:, :128] + result[:, 128:]

    def step(index, carry):
        place = 2 * GROUP * index
        for half in range(2):
            here = place + half * GROUP
            for member in range(GROUP):
                exponents(here + 2 * GROUP + member, gaps[half][member])
                weigh(gaps[1 - half][member], weights[1 - half][member])
                add(here + member, weights[half][member])
        return carry

    return step


def facet_features(
    world_ref, own_ref, out_ref, push_ref, own_force, own_load,
    terms_ref, sem, table, listed, points, force_sum, load_sum, own_sem, *buffers,
):
    keeps = buffers[4 * GROUP + 2 :]
    copy = pltpu.make_async_copy(own_ref.at[pl.ds(48, 8), :], table, own_sem)
    copy.start()
    for keep in keeps:
        keep[...] = jnp.zeros(keep.shape, F32)

    def owner(index, terms_keep, push_keep):
        lever = [world_ref[index, part] for part in range(3)]
        normal = [world_ref[index, 3 + part] for part in range(3)]
        area = world_ref[index, 6]
        last = world_ref[index, 7]
        center = [lever[part] + last[:, part : part + 1] for part in range(3)]
        along = normal[0] * center[0] + normal[1] * center[1] + normal[2] * center[2]
        square = center[0] * center[0] + center[1] * center[1] + center[2] * center[2]
        sides = (
            ([-SHARPNESS * value for value in normal], SHARPNESS * (CONTACT_GAP + along), 0.0),
            ([2.0 * value for value in center], -square, 1.0),
        )
        for side, (factors, constant, tail) in enumerate(sides):
            split = [split3(value) for value in factors]
            order = (0, 1, 2, 0, 1, 0)
            for group, level in enumerate(order):
                for part in range(3):
                    put(terms_keep, side * TERMS + 3 * group + part, split[part][level])
            for level, value in enumerate(split3(constant)):
                put(terms_keep, side * TERMS + 18 + level, value)
                put(terms_keep, side * TERMS + 21 + level, jnp.full((8, 128), tail, F32))
        scaled = (PENALTY / SHARPNESS) * area
        push = [scaled * value for value in normal]
        push.append(lever[1] * push[2] - lever[2] * push[1])
        push.append(lever[2] * push[0] - lever[0] * push[2])
        push.append(lever[0] * push[1] - lever[1] * push[0])
        for part in range(6):
            high = push[part].astype(BF16).astype(F32)
            put(push_keep, part, high)
            put(push_keep, 8 + part, push[part] - high)
        for block in range(BLOCKS):
            both = terms_keep[pl.ds(block, 2 * TERMS, stride=PITCH), :]
            terms_ref[index * BLOCKS + block, 0:128, :] = both[:TERMS].T.astype(BF16)
            terms_ref[index * BLOCKS + block, 128:256, :] = both[TERMS:].T.astype(BF16)
            push_ref[index * BLOCKS + block] = push_keep[
                pl.ds(block, 16, stride=PITCH), :
            ].astype(BF16)

    def owners(index, carry):
        for spare in range(SIDE):
            owner(SIDE * index + spare, *keeps[2 * spare : 2 * spare + 2])
        part = pl.ds(index * SIDE * BLOCKS, SIDE * BLOCKS)
        pltpu.make_async_copy(terms_ref.at[part], out_ref.at[part], sem).start()
        return carry

    lax.fori_loop(0, PLANE // SIDE, owners, 0)
    push_ref[FACETS] = jnp.zeros((16, 128), BF16)
    terms_ref[FACETS] = jnp.zeros((256, TERMS), BF16)
    points[BLOCKS] = jnp.zeros((TERMS, 256), BF16)
    force_sum[...] = jnp.zeros(force_sum.shape, F32)
    load_sum[...] = jnp.zeros(load_sum.shape, F32)
    copy.wait()
    particle_keep = buffers[4 * GROUP : 4 * GROUP + 2]
    for keep in particle_keep:
        keep[...] = jnp.zeros(keep.shape, F32)
    particle_terms(own_ref, points, 0, particle_keep)
    total = table[0, 127].astype(jnp.int32)

    def entry(place, carry):
        listed[2 * GROUP + place] = table[0, place].astype(jnp.int32)
        return carry

    lax.fori_loop(0, total, entry, 0)
    for spare in range(2 * GROUP):
        listed[spare] = BLOCKS * 256 + FACETS
    for spare in range(4 * GROUP):
        listed[2 * GROUP + total + spare] = BLOCKS * 256 + FACETS
    step = pipeline(terms_ref, push_ref, points, listed, force_sum, load_sum, buffers)
    lax.fori_loop(0, (total + 4 * GROUP - 1) // (2 * GROUP), step, 0)
    for block in range(BLOCKS):
        for part in range(3):
            own_force[8 * part + block : 8 * part + block + 1, :] = force_sum[
                block, part : part + 1, :
            ]
    own_load[...] = load_sum[0 : 2 * PLANE]
    done = pltpu.make_async_copy(terms_ref.at[pl.ds(0, FACETS)], out_ref, sem)
    done.wait()


def contact(
    held_ref, push_ref, given_ref, own_force, own_load, force_ref, load_ref,
    terms_ref, held_sem, table, listed, points, force_sum, load_sum,
    sem, *buffers,
):
    copy = pltpu.make_async_copy(given_ref.at[:, pl.ds(48, 8), :], table, sem)
    copy.start()
    held = []
    for part in range(4):
        place = pl.ds(ROW * part, ROW)
        held.append(
            pltpu.make_async_copy(held_ref.at[place], terms_ref.at[place], held_sem.at[part])
        )
        held[-1].start()
    terms_ref[FACETS] = jnp.zeros((256, TERMS), BF16)
    point_keeps = buffers[4 * GROUP :]
    for keep in point_keeps:
        keep[...] = jnp.zeros(keep.shape, F32)
    force_sum[...] = jnp.zeros(force_sum.shape, F32)
    load_sum[0 : 2 * PLANE] = own_load[...]
    load_sum[2 * PLANE] = jnp.zeros((8, 128), F32)
    plane = lax.axis_index("wide") // PLANE
    points[PARTICLES] = jnp.zeros((TERMS, 256), BF16)

    def sources(index, carry):
        for spare in range(SIDE):
            one = SIDE * index + spare
            keeps = point_keeps[2 * spare : 2 * spare + 2]
            particle_terms(given_ref.at[one], points, one * BLOCKS, keeps)
        return carry

    lax.fori_loop(0, DEPTH // SIDE, sources, 0)
    copy.wait()

    def gather(late, start):
        def one(index, start):
            early = table[index, 0, 126].astype(jnp.int32)
            first = jnp.where(late, early, 0)
            count = jnp.where(late, table[index, 0, 127].astype(jnp.int32) - early, early)
            count = jnp.where(index == plane, 0, count)
            shift = index * (BLOCKS * 256)

            def entry(place, carry):
                listed[start + place] = table[index, 0, first + place].astype(jnp.int32) + shift
                return carry

            lax.fori_loop(0, count, entry, 0)
            return start + count

        return lax.fori_loop(0, DEPTH, one, start)

    early = gather(False, 2 * GROUP)
    total = gather(True, early)
    for spare in range(2 * GROUP):
        listed[spare] = PARTICLES * 256 + FACETS
    for spare in range(4 * GROUP):
        listed[total + spare] = PARTICLES * 256 + FACETS

    step = pipeline(terms_ref, push_ref, points, listed, force_sum, load_sum, buffers)
    for one in held[:2]:
        one.wait()
    steps = (early - 2 * GROUP) // (2 * GROUP)
    lax.fori_loop(0, steps, step, 0)
    for one in held[2:]:
        one.wait()
    lax.fori_loop(steps, (total + 2 * GROUP - 1) // (2 * GROUP), step, 0)
    for index in range(DEPTH):
        for block in range(BLOCKS):
            for part in range(3):
                force_ref[index, 8 * part + block : 8 * part + block + 1, :] = force_sum[
                    index * BLOCKS + block, part : part + 1, :
                ]
    force_ref[plane] = own_force[...]
    load_ref[...] = load_sum[0 : 2 * PLANE]


def finish(
    force_ref, velocity_ref, mass_ref, own_ref, other_ref, pose_ref, spin_ref, out_ref, motion_ref,
):
    finish_boulders(own_ref, other_ref, pose_ref, spin_ref, motion_ref)
    total = force_ref[0]
    for index in range(1, DEPTH):
        total = total + force_ref[index]
    scaled = TIME_STEP * mass_ref[...]
    for part in range(3):
        out_ref[part] = velocity_ref[part] + scaled * total[8 * part : 8 * part + 8, :]


def finish_boulders(own_ref, other_ref, pose_ref, velocity_ref, out_ref):
    row = lax.broadcasted_iota(jnp.int32, (2, 6), 0)
    column = lax.broadcasted_iota(jnp.int32, (2, 6), 1)
    change = jnp.zeros((2, 6), F32)
    for boulder in range(2):
        pose = [pose_ref[boulder : boulder + 1, entry : entry + 1] for entry in range(16)]
        total = jnp.sum(own_ref[boulder] + other_ref[boulder], axis=1, keepdims=True)
        force = [-total[part : part + 1, :] for part in range(3)]
        torque = [-total[3 + part : 4 + part, :] for part in range(3)]
        moves = [pose[12] * value for value in force]
        body = []
        for part in range(3):
            turned = (
                pose[3 + part] * torque[0]
                + pose[6 + part] * torque[1]
                + pose[9 + part] * torque[2]
            )
            body.append(turned * pose[13 + part])
        for part in range(3):
            moves.append(
                pose[3 + 3 * part] * body[0]
                + pose[4 + 3 * part] * body[1]
                + pose[5 + 3 * part] * body[2]
            )
        for part in range(6):
            here = jnp.logical_and(row == boulder, column == part)
            change = change + jnp.where(here, moves[part], 0.0)
    out_ref[...] = velocity_ref[...] + TIME_STEP * change


VMEM = pl.BlockSpec(memory_space=pltpu.VMEM)
ANY = pl.BlockSpec(memory_space=pl.ANY)


def call(kernel, outs, in_specs, scratch=(), out_specs=VMEM, limit=VMEM_LIMIT):
    return pl.pallas_call(
        kernel,
        out_shape=outs,
        in_specs=in_specs,
        out_specs=out_specs,
        scratch_shapes=list(scratch),
        compiler_params=pltpu.CompilerParams(vmem_limit_bytes=limit),
    )


def shards(
    particle_position,
    particle_velocity,
    inverse_mass,
    facet_geometry,
    boulder_pose,
    boulder_velocity,
    boulder_slot,
    block_home,
    pair_facet,
    pair_block,
    pair_active,
):
    owners = lax.axis_size("wide")
    planes = [[PLANE * depth + spot for spot in range(PLANE)] for depth in range(owners // PLANE)]
    columns = [[PLANE * depth + spot for depth in range(DEPTH)] for spot in range(PLANE)]
    swap = functools.partial(
        lax.all_to_all, axis_name="wide", split_axis=0, concat_axis=0, tiled=True
    )
    pairs = pair_facet.shape[0]
    shape = jax.ShapeDtypeStruct

    def shift(step, unit):
        moves = []
        for device in range(owners):
            place = device // unit % 4
            moves.append((device, device + ((place + step) % 4 - place) * unit))
        return moves

    geometry = facet_geometry.transpose(0, 2, 1, 3)
    facets = call(
        facet_message,
        shape((PLANE, 8, BLOCKS, 128), F32),
        [ANY, ANY],
        [
            pltpu.VMEM(geometry.shape, F32),
            pltpu.SMEM(boulder_pose.shape, F32),
            pltpu.SemaphoreType.DMA((2,)),
        ],
        limit=WHOLE_VMEM,
    )(geometry, boulder_pose)
    facets = swap(facets, axis_index_groups=planes)
    lists = [
        particle_position.transpose(1, 0, 2),
        boulder_slot.reshape(-1, 128),
        block_home.reshape(-1, 128),
        pair_facet.reshape(1, pairs),
        pair_block.reshape(1, pairs),
        pair_active.reshape(1, pairs),
    ]
    particles, own = call(
        pair_message,
        [shape((DEPTH, 56, 128), F32), shape((56, 128), F32)],
        [ANY] * 6,
        [pltpu.VMEM(value.shape, value.dtype) for value in lists]
        + [pltpu.SemaphoreType.DMA((6,))],
        out_specs=[VMEM, VMEM],
        limit=WHOLE_VMEM,
    )(*lists)
    work = [pltpu.VMEM((256, 256), F32)] * (2 * GROUP) + [pltpu.VMEM((256, 256), BF16)] * (2 * GROUP)
    terms, push, own_force, own_load = call(
        facet_features,
        [
            shape((FACETS, 256, TERMS), BF16),
            shape((FACETS + 1, 16, 128), BF16),
            shape((24, 256), F32),
            shape((2 * PLANE, 8, 128), F32),
        ],
        [VMEM, VMEM],
        [
            pltpu.VMEM((FACETS + 1, 256, TERMS), BF16),
            pltpu.SemaphoreType.DMA,
            pltpu.SMEM((8, 128), F32),
            pltpu.SMEM((48 + 6 * GROUP,), jnp.int32),
            pltpu.VMEM((BLOCKS + 1, TERMS, 256), BF16),
            pltpu.VMEM((BLOCKS + 1, 8, 256), F32),
            pltpu.VMEM((2 * PLANE + 1, 8, 128), F32),
            pltpu.SemaphoreType.DMA,
        ]
        + work
        + [pltpu.VMEM((TERMS * PITCH, 128), F32)] * 2
        + [pltpu.VMEM((2 * TERMS * PITCH, 128), F32), pltpu.VMEM((16 * PITCH, 128), F32)] * SIDE,
        out_specs=[ANY, VMEM, VMEM, VMEM],
    )(facets, own)
    particles = swap(particles, axis_index_groups=columns)
    force, load = call(
        contact,
        [shape((DEPTH, 24, 256), F32), shape((2 * PLANE, 8, 128), F32)],
        [ANY] + [VMEM] * 4,
        [
            pltpu.VMEM((FACETS + 1, 256, TERMS), BF16),
            pltpu.SemaphoreType.DMA((4,)),
            pltpu.SMEM((DEPTH, 8, 128), F32),
            pltpu.SMEM((DEPTH * 48 + 6 * GROUP,), jnp.int32),
            pltpu.VMEM((PARTICLES + 1, TERMS, 256), BF16),
            pltpu.VMEM((PARTICLES + 1, 8, 256), F32),
            pltpu.VMEM((2 * PLANE + 1, 8, 128), F32),
            pltpu.SemaphoreType.DMA,
        ]
        + work
        + [pltpu.VMEM((TERMS * PITCH, 128), F32)] * (2 * SIDE),
        out_specs=[VMEM, VMEM],
    )(terms, push, particles, own_force, own_load)
    grid = load.reshape(4, 4, 2, 8, 128)
    spot = lax.axis_index("wide") % PLANE
    down, across = spot // 4, spot % 4
    def pick(array, axis, index):
        return lax.dynamic_index_in_dim(array, index % 4, axis, keepdims=False)

    row = pick(grid, 1, across)
    for step in (1, 2, 3):
        row = row + lax.ppermute(pick(grid, 1, across + step), "wide", shift(step, 1))
    load = pick(row, 0, down)
    for step in (1, 2, 3):
        load = load + lax.ppermute(pick(row, 0, down + step), "wide", shift(step, 4))
    other = lax.ppermute(load, "narrow", [(0, 1), (1, 0)])
    force = swap(force, axis_index_groups=columns)
    velocity = particle_velocity.transpose(1, 0, 2)
    new_velocity, boulder_motion = call(
        finish,
        [shape(velocity.shape, F32), shape(boulder_velocity.shape, F32)],
        [VMEM] * 7,
        out_specs=[VMEM, VMEM],
    )(force, velocity, inverse_mass, load, other, boulder_pose, boulder_velocity)
    return (new_velocity.transpose(1, 0, 2), boulder_motion)


def solution(mesh):
    return jax.shard_map(
        shards,
        mesh=mesh,
        in_specs=(
            P(("wide", "narrow"), None, None),
            P(("wide", "narrow"), None, None),
            P(("wide", "narrow"), None),
            P("wide", None, None, None),
            P("wide", None),
            P("wide", None),
            P(),
            P(),
            P(("wide", "narrow")),
            P(("wide", "narrow")),
            P(("wide", "narrow")),
        ),
        out_specs=(P(("wide", "narrow"), None, None), P("wide", None)),
        check_vma=False,
    )
```

```python
import functools

import jax
import jax.numpy as jnp
from jax import lax
from jax.experimental import pallas as pl
from jax.experimental.pallas import tpu as pltpu
from jax.sharding import PartitionSpec as P

PENALTY = 0.3
SHARPNESS = 4.0
CONTACT_GAP = 0.1
TIME_STEP = 0.5

PLANE = 16
DEPTH = 8
BLOCKS = 8
TERMS = 32
PITCH = 9
FACETS = PLANE * BLOCKS
ROW = 4 * BLOCKS
PARTICLES = DEPTH * BLOCKS
GROUP = 2
FAR = 1e15
SIDE = 4
VMEM_LIMIT = 48 * 1024 * 1024
WHOLE_VMEM = 63 * 1024 * 1024

F32 = jnp.float32
BF16 = jnp.bfloat16


def split3(value):
    high = value.astype(BF16).astype(F32)
    rest = value - high
    middle = rest.astype(BF16).astype(F32)
    return high, middle, (rest - middle).astype(BF16).astype(F32)


def put(keep, row, value):
    keep[PITCH * row : PITCH * row + BLOCKS, :] = value


def fetch(pairs, sems):
    copies = [
        pltpu.make_async_copy(origin, target, sems.at[index])
        for index, (origin, target) in enumerate(pairs)
    ]
    for copy in copies:
        copy.start()
    for copy in copies:
        copy.wait()


def facet_message(geometry_at, pose_at, out_ref, geometry_ref, pose_ref, sems):
    fetch([(geometry_at, geometry_ref), (pose_at, pose_ref)], sems)
    lane = lax.broadcasted_iota(jnp.int32, (4, 128), 1)
    for boulder in range(2):
        part = [geometry_ref[boulder, row] for row in range(7)]
        center = [pose_ref[boulder, row] for row in range(3)]
        rotation = [pose_ref[boulder, 3 + entry] for entry in range(9)]
        rows = []
        for first in (0, 3):
            for row in range(3):
                rows.append(
                    rotation[3 * row] * part[first]
                    + rotation[3 * row + 1] * part[first + 1]
                    + rotation[3 * row + 2] * part[first + 2]
                )
        rows.append(part[6])
        rows.append(
            jnp.where(
                lane == 0,
                center[0],
                jnp.where(lane == 1, center[1], jnp.where(lane == 2, center[2], 0.0)),
            )
        )
        for target in range(PLANE):
            for row in range(8):
                out_ref[target, row, 4 * boulder : 4 * boulder + 4, :] = rows[row]


def pair_message(*refs):
    held, (out_ref, own_ref), (position_ref, slot_ref, home_ref), rows, sems = (
        refs[:6], refs[6:8], refs[8:11], refs[11:14], refs[14],
    )
    fetch(list(zip(held, (position_ref, slot_ref, home_ref, *rows))), sems)
    facet, block, active = [row[...] for row in rows]
    pairs = facet.shape[1]
    packed = jnp.where(active != 0, 1, 0) + 2 * facet + 2048 * block
    packed = jnp.broadcast_to(packed, (128, pairs)).T[:, 0:1]
    active = (packed & 1) != 0
    facet = (packed >> 1) & 1023
    block = packed >> 11
    lane = lax.broadcasted_iota(jnp.int32, (pairs, 128), 1)

    def look_up(table, index):
        rows = table.shape[0]
        row = lax.broadcasted_iota(jnp.int32, (pairs, rows), 1)
        onehot = ((index >> 7) == row).astype(F32).astype(BF16)
        picked = jnp.dot(onehot, table.astype(F32).astype(BF16), preferred_element_type=F32)
        picked = jnp.where(lane == (index & 127), picked, 0.0)
        return jnp.sum(picked, axis=1, keepdims=True).astype(jnp.int32)

    slot = look_up(slot_ref[...], facet >> 2)
    local_block = look_up(home_ref[...] & 7, block)
    plane = slot >> 5
    code = local_block * 256 + ((slot & 31) * 4 + (facet & 3))
    code = code.astype(F32)
    late = (slot >> 3) & 2
    member = jnp.logical_and(lane == plane + DEPTH * (late >> 1), active).astype(F32)
    row = lax.broadcasted_iota(jnp.int32, (pairs, pairs), 0)
    column = lax.broadcasted_iota(jnp.int32, (pairs, pairs), 1)
    below = (column < row).astype(F32).astype(BF16)
    before = jnp.dot(below, member.astype(BF16), preferred_element_type=F32)
    rank = jnp.sum(before * member, axis=1, keepdims=True)
    early = jnp.sum(member, axis=0, keepdims=True)
    ahead = jnp.where(jnp.logical_and(lane == plane, late > 0), early, 0.0)
    rank = (rank + jnp.sum(ahead, axis=1, keepdims=True)).astype(jnp.int32)
    rank = jnp.where(active, rank, 255)
    spread = jnp.where(lane == rank, code, 0.0)
    lane_row = lax.broadcasted_iota(jnp.int32, (1, 128), 1)
    for target in range(DEPTH):
        here = jnp.logical_and(plane == target, active)
        listed = jnp.sum(jnp.where(here, spread, 0.0), axis=0, keepdims=True)
        count = jnp.sum(here.astype(F32), axis=0, keepdims=True)
        first = jnp.sum(jnp.where(lane_row == target, early, 0.0), axis=1, keepdims=True)
        listed = jnp.where(lane_row == 126, first, jnp.where(lane_row == 127, count, listed))
        for half in range(2):
            for part in range(3):
                first = 24 * half + 8 * part
                out_ref[target, first : first + 8, :] = position_ref[
                    part, :, 128 * half : 128 * half + 128
                ]
        out_ref[target, 48:56, :] = jnp.broadcast_to(listed, (8, 128))
    own_ref[...] = out_ref[lax.axis_index("wide") // PLANE]


def particle_terms(place_ref, points, first, point_keep):
    for half in range(2):
        keep = point_keep[half]
        place = [
            place_ref[24 * half + 8 * part : 24 * half + 8 * part + 8, :]
            for part in range(3)
        ]
        square = place[0] * place[0] + place[1] * place[1] + place[2] * place[2]
        split = [split3(value) for value in place]
        for group, level in enumerate((0, 0, 0, 1, 1, 2)):
            for part in range(3):
                put(keep, 3 * group + part, split[part][level])
        for level, value in enumerate(split3(-square)):
            put(keep, 18 + level, jnp.full((8, 128), 1.0, F32))
            put(keep, 21 + level, value)
    for block in range(BLOCKS):
        for half in range(2):
            points[first + block, :, 128 * half : 128 * half + 128] = point_keep[half][
                pl.ds(block, TERMS, stride=PITCH), :
            ].astype(BF16)


def pipeline(terms_ref, push_ref, points, listed, force_sum, load_sum, buffers):
    gaps = [buffers[0:GROUP], buffers[GROUP : 2 * GROUP]]
    weights = [buffers[2 * GROUP : 3 * GROUP], buffers[3 * GROUP : 4 * GROUP]]

    def exponents(place, buffer):
        code = listed[place]
        buffer[...] = jnp.dot(
            terms_ref[code & 255], points[code >> 8], preferred_element_type=F32
        )

    def weigh(buffer, weight_ref):
        for first in range(0, 128, 16):
            gap = buffer[first : first + 16, :]
            soft = jnp.where(gap > 80.0, gap, jnp.log(1.0 + jnp.exp(gap)))
            weight = jnp.exp(buffer[128 + first : 144 + first, :]) * soft
            high = weight.astype(BF16)
            weight_ref[first : first + 16, :] = high
            weight_ref[128 + first : 144 + first, :] = (weight - high.astype(F32)).astype(BF16)

    def add(place, weight_ref):
        code = listed[place]
        facet = code & 255
        push = push_ref[facet]
        result = jnp.dot(
            jnp.concatenate([push, push], axis=1), weight_ref[...], preferred_element_type=F32
        )
        result = result[0:8] + result[8:16]
        force_sum[code >> 8] += result
        load_sum[facet >> 2] += result[:, :128] + result[:, 128:]

    def step(index, carry):
        place = 2 * GROUP * index
        for half in range(2):
            here = place + half * GROUP
            for member in range(GROUP):
                exponents(here + 2 * GROUP + member, gaps[half][member])
                weigh(gaps[1 - half][member], weights[1 - half][member])
                add(here + member, weights[half][member])
        return carry

    return step


def facet_features(
    world_ref, own_ref, out_ref, push_ref, own_force, own_load,
    terms_ref, sem, table, listed, points, force_sum, load_sum, own_sem, *buffers,
):
    keeps = buffers[4 * GROUP + 2 :]
    copy = pltpu.make_async_copy(own_ref.at[pl.ds(48, 8), :], table, own_sem)
    copy.start()
    for keep in keeps:
        keep[...] = jnp.zeros(keep.shape, F32)

    def owner(index, terms_keep, push_keep):
        lever = [world_ref[index, part] for part in range(3)]
        normal = [world_ref[index, 3 + part] for part in range(3)]
        area = world_ref[index, 6]
        last = world_ref[index, 7]
        center = [
            jnp.clip(lever[part] + last[:, part : part + 1], -FAR, FAR) for part in range(3)
        ]
        along = normal[0] * center[0] + normal[1] * center[1] + normal[2] * center[2]
        square = center[0] * center[0] + center[1] * center[1] + center[2] * center[2]
        sides = (
            ([-SHARPNESS * value for value in normal], SHARPNESS * (CONTACT_GAP + along), 0.0),
            ([2.0 * value for value in center], -square, 1.0),
        )
        for side, (factors, constant, tail) in enumerate(sides):
            split = [split3(value) for value in factors]
            order = (0, 1, 2, 0, 1, 0)
            for group, level in enumerate(order):
                for part in range(3):
                    put(terms_keep, side * TERMS + 3 * group + part, split[part][level])
            for level, value in enumerate(split3(constant)):
                put(terms_keep, side * TERMS + 18 + level, value)
                put(terms_keep, side * TERMS + 21 + level, jnp.full((8, 128), tail, F32))
        scaled = (PENALTY / SHARPNESS) * area
        push = [scaled * value for value in normal]
        push.append(lever[1] * push[2] - lever[2] * push[1])
        push.append(lever[2] * push[0] - lever[0] * push[2])
        push.append(lever[0] * push[1] - lever[1] * push[0])
        for part in range(6):
            high = push[part].astype(BF16).astype(F32)
            put(push_keep, part, high)
            put(push_keep, 8 + part, push[part] - high)
        for block in range(BLOCKS):
            both = terms_keep[pl.ds(block, 2 * TERMS, stride=PITCH), :]
            terms_ref[index * BLOCKS + block, 0:128, :] = both[:TERMS].T.astype(BF16)
            terms_ref[index * BLOCKS + block, 128:256, :] = both[TERMS:].T.astype(BF16)
            push_ref[index * BLOCKS + block] = push_keep[
                pl.ds(block, 16, stride=PITCH), :
            ].astype(BF16)

    def owners(index, carry):
        for spare in range(SIDE):
            owner(SIDE * index + spare, *keeps[2 * spare : 2 * spare + 2])
        part = pl.ds(index * SIDE * BLOCKS, SIDE * BLOCKS)
        pltpu.make_async_copy(terms_ref.at[part], out_ref.at[part], sem).start()
        return carry

    lax.fori_loop(0, PLANE // SIDE, owners, 0)
    push_ref[FACETS] = jnp.zeros((16, 128), BF16)
    terms_ref[FACETS] = jnp.zeros((256, TERMS), BF16)
    points[BLOCKS] = jnp.zeros((TERMS, 256), BF16)
    force_sum[...] = jnp.zeros(force_sum.shape, F32)
    load_sum[...] = jnp.zeros(load_sum.shape, F32)
    copy.wait()
    particle_keep = buffers[4 * GROUP : 4 * GROUP + 2]
    for keep in particle_keep:
        keep[...] = jnp.zeros(keep.shape, F32)
    particle_terms(own_ref, points, 0, particle_keep)
    total = table[0, 127].astype(jnp.int32)

    def entry(step, carry):
        for spare in range(4):
            place = 4 * step + spare
            listed[2 * GROUP + place] = table[0, place].astype(jnp.int32)
        return carry

    lax.fori_loop(0, (total + 3) // 4, entry, 0)
    for spare in range(2 * GROUP):
        listed[spare] = BLOCKS * 256 + FACETS
    for spare in range(4 * GROUP):
        listed[2 * GROUP + total + spare] = BLOCKS * 256 + FACETS
    step = pipeline(terms_ref, push_ref, points, listed, force_sum, load_sum, buffers)
    lax.fori_loop(0, (total + 4 * GROUP - 1) // (2 * GROUP), step, 0)
    for block in range(BLOCKS):
        for part in range(3):
            own_force[8 * part + block : 8 * part + block + 1, :] = force_sum[
                block, part : part + 1, :
            ]
    own_load[...] = load_sum[0 : 2 * PLANE]
    done = pltpu.make_async_copy(terms_ref.at[pl.ds(0, FACETS)], out_ref, sem)
    done.wait()


def contact(
    held_ref, push_ref, given_ref, own_force, own_load, force_ref, load_ref,
    terms_ref, held_sem, table, listed, points, force_sum, load_sum,
    sem, *buffers,
):
    copy = pltpu.make_async_copy(given_ref.at[:, pl.ds(48, 8), :], table, sem)
    copy.start()
    held = []
    for part in range(4):
        place = pl.ds(ROW * part, ROW)
        held.append(
            pltpu.make_async_copy(held_ref.at[place], terms_ref.at[place], held_sem.at[part])
        )
        held[-1].start()
    terms_ref[FACETS] = jnp.zeros((256, TERMS), BF16)
    point_keeps = buffers[4 * GROUP :]
    for keep in point_keeps:
        keep[...] = jnp.zeros(keep.shape, F32)
    force_sum[...] = jnp.zeros(force_sum.shape, F32)
    load_sum[0 : 2 * PLANE] = own_load[...]
    load_sum[2 * PLANE] = jnp.zeros((8, 128), F32)
    plane = lax.axis_index("wide") // PLANE
    points[PARTICLES] = jnp.zeros((TERMS, 256), BF16)

    def sources(index, carry):
        for spare in range(SIDE):
            one = SIDE * index + spare
            keeps = point_keeps[2 * spare : 2 * spare + 2]
            particle_terms(given_ref.at[one], points, one * BLOCKS, keeps)
        return carry

    lax.fori_loop(0, DEPTH // SIDE, sources, 0)
    copy.wait()

    def gather(late, start):
        def one(index, start):
            early = table[index, 0, 126].astype(jnp.int32)
            first = jnp.where(late, early, 0)
            count = jnp.where(late, table[index, 0, 127].astype(jnp.int32) - early, early)
            count = jnp.where(index == plane, 0, count)
            shift = index * (BLOCKS * 256)

            def entry(step, carry):
                for spare in range(4):
                    place = 4 * step + spare
                    listed[start + place] = table[index, 0, first + place].astype(jnp.int32) + shift
                return carry

            lax.fori_loop(0, (count + 3) // 4, entry, 0)
            return start + count

        return lax.fori_loop(0, DEPTH, one, start)

    early = gather(False, 2 * GROUP)
    total = gather(True, early)
    for spare in range(2 * GROUP):
        listed[spare] = PARTICLES * 256 + FACETS
    for spare in range(4 * GROUP):
        listed[total + spare] = PARTICLES * 256 + FACETS

    step = pipeline(terms_ref, push_ref, points, listed, force_sum, load_sum, buffers)
    for one in held[:2]:
        one.wait()
    steps = (early - 2 * GROUP) // (2 * GROUP)
    lax.fori_loop(0, steps, step, 0)
    for one in held[2:]:
        one.wait()
    lax.fori_loop(steps, (total + 2 * GROUP - 1) // (2 * GROUP), step, 0)
    for index in range(DEPTH):
        for block in range(BLOCKS):
            for part in range(3):
                force_ref[index, 8 * part + block : 8 * part + block + 1, :] = force_sum[
                    index * BLOCKS + block, part : part + 1, :
                ]
    force_ref[plane] = own_force[...]
    load_ref[...] = load_sum[0 : 2 * PLANE]


def finish(
    force_ref, velocity_ref, mass_ref, own_ref, other_ref, pose_ref, spin_ref, out_ref, motion_ref,
):
    finish_boulders(own_ref, other_ref, pose_ref, spin_ref, motion_ref)
    total = force_ref[0]
    for index in range(1, DEPTH):
        total = total + force_ref[index]
    scaled = TIME_STEP * mass_ref[...]
    for part in range(3):
        out_ref[part] = velocity_ref[part] + scaled * total[8 * part : 8 * part + 8, :]


def finish_boulders(own_ref, other_ref, pose_ref, velocity_ref, out_ref):
    row = lax.broadcasted_iota(jnp.int32, (2, 6), 0)
    column = lax.broadcasted_iota(jnp.int32, (2, 6), 1)
    change = jnp.zeros((2, 6), F32)
    for boulder in range(2):
        pose = [pose_ref[boulder : boulder + 1, entry : entry + 1] for entry in range(16)]
        total = jnp.sum(own_ref[boulder] + other_ref[boulder], axis=1, keepdims=True)
        force = [-total[part : part + 1, :] for part in range(3)]
        torque = [-total[3 + part : 4 + part, :] for part in range(3)]
        moves = [pose[12] * value for value in force]
        body = []
        for part in range(3):
            turned = (
                pose[3 + part] * torque[0]
                + pose[6 + part] * torque[1]
                + pose[9 + part] * torque[2]
            )
            body.append(turned * pose[13 + part])
        for part in range(3):
            moves.append(
                pose[3 + 3 * part] * body[0]
                + pose[4 + 3 * part] * body[1]
                + pose[5 + 3 * part] * body[2]
            )
        for part in range(6):
            here = jnp.logical_and(row == boulder, column == part)
            change = change + jnp.where(here, moves[part], 0.0)
    out_ref[...] = velocity_ref[...] + TIME_STEP * change


VMEM = pl.BlockSpec(memory_space=pltpu.VMEM)
ANY = pl.BlockSpec(memory_space=pl.ANY)


def call(kernel, outs, in_specs, scratch=(), out_specs=VMEM, limit=VMEM_LIMIT):
    return pl.pallas_call(
        kernel,
        out_shape=outs,
        in_specs=in_specs,
        out_specs=out_specs,
        scratch_shapes=list(scratch),
        compiler_params=pltpu.CompilerParams(vmem_limit_bytes=limit),
    )


def shards(
    particle_position,
    particle_velocity,
    inverse_mass,
    facet_geometry,
    boulder_pose,
    boulder_velocity,
    boulder_slot,
    block_home,
    pair_facet,
    pair_block,
    pair_active,
):
    owners = lax.axis_size("wide")
    planes = [[PLANE * depth + spot for spot in range(PLANE)] for depth in range(owners // PLANE)]
    columns = [[PLANE * depth + spot for depth in range(DEPTH)] for spot in range(PLANE)]
    swap = functools.partial(
        lax.all_to_all, axis_name="wide", split_axis=0, concat_axis=0, tiled=True
    )
    pairs = pair_facet.shape[0]
    shape = jax.ShapeDtypeStruct

    def shift(step, unit):
        moves = []
        for device in range(owners):
            place = device // unit % 4
            moves.append((device, device + ((place + step) % 4 - place) * unit))
        return moves

    geometry = facet_geometry.transpose(0, 2, 1, 3)
    facets = call(
        facet_message,
        shape((PLANE, 8, BLOCKS, 128), F32),
        [ANY, ANY],
        [
            pltpu.VMEM(geometry.shape, F32),
            pltpu.SMEM(boulder_pose.shape, F32),
            pltpu.SemaphoreType.DMA((2,)),
        ],
        limit=WHOLE_VMEM,
    )(geometry, boulder_pose)
    facets = swap(facets, axis_index_groups=planes)
    lists = [
        particle_position.transpose(1, 0, 2),
        boulder_slot.reshape(-1, 128),
        block_home.reshape(-1, 128),
        pair_facet.reshape(1, pairs),
        pair_block.reshape(1, pairs),
        pair_active.reshape(1, pairs),
    ]
    particles, own = call(
        pair_message,
        [shape((DEPTH, 56, 128), F32), shape((56, 128), F32)],
        [ANY] * 6,
        [pltpu.VMEM(value.shape, value.dtype) for value in lists]
        + [pltpu.SemaphoreType.DMA((6,))],
        out_specs=[VMEM, VMEM],
        limit=WHOLE_VMEM,
    )(*lists)
    work = [pltpu.VMEM((256, 256), F32)] * (2 * GROUP) + [pltpu.VMEM((256, 256), BF16)] * (2 * GROUP)
    terms, push, own_force, own_load = call(
        facet_features,
        [
            shape((FACETS, 256, TERMS), BF16),
            shape((FACETS + 1, 16, 128), BF16),
            shape((24, 256), F32),
            shape((2 * PLANE, 8, 128), F32),
        ],
        [VMEM, VMEM],
        [
            pltpu.VMEM((FACETS + 1, 256, TERMS), BF16),
            pltpu.SemaphoreType.DMA,
            pltpu.SMEM((8, 128), F32),
            pltpu.SMEM((48 + 6 * GROUP,), jnp.int32),
            pltpu.VMEM((BLOCKS + 1, TERMS, 256), BF16),
            pltpu.VMEM((BLOCKS + 1, 8, 256), F32),
            pltpu.VMEM((2 * PLANE + 1, 8, 128), F32),
            pltpu.SemaphoreType.DMA,
        ]
        + work
        + [pltpu.VMEM((TERMS * PITCH, 128), F32)] * 2
        + [pltpu.VMEM((2 * TERMS * PITCH, 128), F32), pltpu.VMEM((16 * PITCH, 128), F32)] * SIDE,
        out_specs=[ANY, VMEM, VMEM, VMEM],
    )(facets, own)
    particles = swap(particles, axis_index_groups=columns)
    force, load = call(
        contact,
        [shape((DEPTH, 24, 256), F32), shape((2 * PLANE, 8, 128), F32)],
        [ANY] + [VMEM] * 4,
        [
            pltpu.VMEM((FACETS + 1, 256, TERMS), BF16),
            pltpu.SemaphoreType.DMA((4,)),
            pltpu.SMEM((DEPTH, 8, 128), F32),
            pltpu.SMEM((DEPTH * 48 + 6 * GROUP,), jnp.int32),
            pltpu.VMEM((PARTICLES + 1, TERMS, 256), BF16),
            pltpu.VMEM((PARTICLES + 1, 8, 256), F32),
            pltpu.VMEM((2 * PLANE + 1, 8, 128), F32),
            pltpu.SemaphoreType.DMA,
        ]
        + work
        + [pltpu.VMEM((TERMS * PITCH, 128), F32)] * (2 * SIDE),
        out_specs=[VMEM, VMEM],
    )(terms, push, particles, own_force, own_load)
    grid = load.reshape(4, 4, 2, 8, 128)
    spot = lax.axis_index("wide") % PLANE
    down, across = spot // 4, spot % 4
    def pick(array, axis, index):
        return lax.dynamic_index_in_dim(array, index % 4, axis, keepdims=False)

    row = pick(grid, 1, across)
    for step in (1, 2, 3):
        row = row + lax.ppermute(pick(grid, 1, across + step), "wide", shift(step, 1))
    load = pick(row, 0, down)
    for step in (1, 2, 3):
        load = load + lax.ppermute(pick(row, 0, down + step), "wide", shift(step, 4))
    other = lax.ppermute(load, "narrow", [(0, 1), (1, 0)])
    force = swap(force, axis_index_groups=columns)
    velocity = particle_velocity.transpose(1, 0, 2)
    new_velocity, boulder_motion = call(
        finish,
        [shape(velocity.shape, F32), shape(boulder_velocity.shape, F32)],
        [VMEM] * 7,
        out_specs=[VMEM, VMEM],
    )(force, velocity, inverse_mass, load, other, boulder_pose, boulder_velocity)
    return (new_velocity.transpose(1, 0, 2), boulder_motion)


def solution(mesh):
    return jax.shard_map(
        shards,
        mesh=mesh,
        in_specs=(
            P(("wide", "narrow"), None, None),
            P(("wide", "narrow"), None, None),
            P(("wide", "narrow"), None),
            P("wide", None, None, None),
            P("wide", None),
            P("wide", None),
            P(),
            P(),
            P(("wide", "narrow")),
            P(("wide", "narrow")),
            P(("wide", "narrow")),
        ),
        out_specs=(P(("wide", "narrow"), None, None), P("wide", None)),
        check_vma=False,
    )
```

```python
import functools

import jax
import jax.numpy as jnp
from jax import lax
from jax.experimental import pallas as pl
from jax.experimental.pallas import tpu as pltpu
from jax.sharding import PartitionSpec as P

PENALTY = 0.3
SHARPNESS = 4.0
CONTACT_GAP = 0.1
TIME_STEP = 0.5

PLANE = 16
DEPTH = 8
BLOCKS = 8
TERMS = 32
PITCH = 9
FACETS = PLANE * BLOCKS
ROW = 4 * BLOCKS
PARTICLES = DEPTH * BLOCKS
GROUP = 2
FAR = 1e15
SIDE = 8
VMEM_LIMIT = 48 * 1024 * 1024
WHOLE_VMEM = 63 * 1024 * 1024

F32 = jnp.float32
BF16 = jnp.bfloat16


def split3(value):
    high = value.astype(BF16).astype(F32)
    rest = value - high
    middle = rest.astype(BF16).astype(F32)
    return high, middle, (rest - middle).astype(BF16).astype(F32)


def put(keep, row, value):
    keep[PITCH * row : PITCH * row + BLOCKS, :] = value


def fetch(pairs, sems):
    copies = [
        pltpu.make_async_copy(origin, target, sems.at[index])
        for index, (origin, target) in enumerate(pairs)
    ]
    for copy in copies:
        copy.start()
    for copy in copies:
        copy.wait()


def facet_message(geometry_at, pose_at, out_ref, geometry_ref, pose_ref, sems):
    fetch([(geometry_at, geometry_ref), (pose_at, pose_ref)], sems)
    lane = lax.broadcasted_iota(jnp.int32, (4, 128), 1)
    for boulder in range(2):
        part = [geometry_ref[boulder, row] for row in range(7)]
        center = [pose_ref[boulder, row] for row in range(3)]
        rotation = [pose_ref[boulder, 3 + entry] for entry in range(9)]
        rows = []
        for first in (0, 3):
            for row in range(3):
                rows.append(
                    rotation[3 * row] * part[first]
                    + rotation[3 * row + 1] * part[first + 1]
                    + rotation[3 * row + 2] * part[first + 2]
                )
        rows.append(part[6])
        rows.append(
            jnp.where(
                lane == 0,
                center[0],
                jnp.where(lane == 1, center[1], jnp.where(lane == 2, center[2], 0.0)),
            )
        )
        for target in range(PLANE):
            for row in range(8):
                out_ref[target, row, 4 * boulder : 4 * boulder + 4, :] = rows[row]


def pair_message(*refs):
    held, (out_ref, own_ref), (position_ref, slot_ref, home_ref), rows, sems = (
        refs[:6], refs[6:8], refs[8:11], refs[11:14], refs[14],
    )
    fetch(list(zip(held, (position_ref, slot_ref, home_ref, *rows))), sems)
    facet, block, active = [row[...] for row in rows]
    pairs = facet.shape[1]
    packed = jnp.where(active != 0, 1, 0) + 2 * facet + 2048 * block
    packed = jnp.broadcast_to(packed, (128, pairs)).T[:, 0:1]
    active = (packed & 1) != 0
    facet = (packed >> 1) & 1023
    block = packed >> 11
    lane = lax.broadcasted_iota(jnp.int32, (pairs, 128), 1)

    def look_up(table, index):
        rows = table.shape[0]
        row = lax.broadcasted_iota(jnp.int32, (pairs, rows), 1)
        onehot = ((index >> 7) == row).astype(F32).astype(BF16)
        picked = jnp.dot(onehot, table.astype(F32).astype(BF16), preferred_element_type=F32)
        picked = jnp.where(lane == (index & 127), picked, 0.0)
        return jnp.sum(picked, axis=1, keepdims=True).astype(jnp.int32)

    slot = look_up(slot_ref[...], facet >> 2)
    local_block = look_up(home_ref[...] & 7, block)
    plane = slot >> 5
    code = local_block * 256 + ((slot & 31) * 4 + (facet & 3))
    code = code.astype(F32)
    late = (slot >> 3) & 2
    member = jnp.logical_and(lane == plane + DEPTH * (late >> 1), active).astype(F32)
    row = lax.broadcasted_iota(jnp.int32, (pairs, pairs), 0)
    column = lax.broadcasted_iota(jnp.int32, (pairs, pairs), 1)
    below = (column < row).astype(F32).astype(BF16)
    before = jnp.dot(below, member.astype(BF16), preferred_element_type=F32)
    rank = jnp.sum(before * member, axis=1, keepdims=True)
    early = jnp.sum(member, axis=0, keepdims=True)
    ahead = jnp.where(jnp.logical_and(lane == plane, late > 0), early, 0.0)
    rank = (rank + jnp.sum(ahead, axis=1, keepdims=True)).astype(jnp.int32)
    rank = jnp.where(active, rank, 255)
    spread = jnp.where(lane == rank, code, 0.0)
    lane_row = lax.broadcasted_iota(jnp.int32, (1, 128), 1)
    for target in range(DEPTH):
        here = jnp.logical_and(plane == target, active)
        listed = jnp.sum(jnp.where(here, spread, 0.0), axis=0, keepdims=True)
        count = jnp.sum(here.astype(F32), axis=0, keepdims=True)
        first = jnp.sum(jnp.where(lane_row == target, early, 0.0), axis=1, keepdims=True)
        listed = jnp.where(lane_row == 126, first, jnp.where(lane_row == 127, count, listed))
        for half in range(2):
            for part in range(3):
                first = 24 * half + 8 * part
                out_ref[target, first : first + 8, :] = position_ref[
                    part, :, 128 * half : 128 * half + 128
                ]
        out_ref[target, 48:56, :] = jnp.broadcast_to(listed, (8, 128))
    own_ref[...] = out_ref[lax.axis_index("wide") // PLANE]


def particle_terms(place_ref, points, first, point_keep):
    for half in range(2):
        keep = point_keep[half]
        place = [
            place_ref[24 * half + 8 * part : 24 * half + 8 * part + 8, :]
            for part in range(3)
        ]
        square = place[0] * place[0] + place[1] * place[1] + place[2] * place[2]
        split = [split3(value) for value in place]
        for group, level in enumerate((0, 0, 0, 1, 1, 2)):
            for part in range(3):
                put(keep, 3 * group + part, split[part][level])
        for level, value in enumerate(split3(-square)):
            put(keep, 18 + level, jnp.full((8, 128), 1.0, F32))
            put(keep, 21 + level, value)
    for block in range(BLOCKS):
        for half in range(2):
            points[first + block, :, 128 * half : 128 * half + 128] = point_keep[half][
                pl.ds(block, TERMS, stride=PITCH), :
            ].astype(BF16)


def pipeline(terms_ref, push_ref, points, listed, force_sum, load_sum, buffers):
    gaps = [buffers[0:GROUP], buffers[GROUP : 2 * GROUP]]
    weights = [buffers[2 * GROUP : 3 * GROUP], buffers[3 * GROUP : 4 * GROUP]]

    def exponents(place, buffer):
        code = listed[place]
        buffer[...] = jnp.dot(
            terms_ref[code & 255], points[code >> 8], preferred_element_type=F32
        )

    def weigh(buffer, weight_ref):
        for first in range(0, 128, 16):
            gap = buffer[first : first + 16, :]
            soft = jnp.where(gap > 80.0, gap, jnp.log(1.0 + jnp.exp(gap)))
            weight = jnp.exp(buffer[128 + first : 144 + first, :]) * soft
            high = weight.astype(BF16)
            weight_ref[first : first + 16, :] = high
            weight_ref[128 + first : 144 + first, :] = (weight - high.astype(F32)).astype(BF16)

    def add(place, weight_ref):
        code = listed[place]
        facet = code & 255
        push = push_ref[facet]
        result = jnp.dot(
            jnp.concatenate([push, push], axis=1), weight_ref[...], preferred_element_type=F32
        )
        result = result[0:8] + result[8:16]
        force_sum[code >> 8] += result
        load_sum[facet >> 2] += result[:, :128] + result[:, 128:]

    def step(index, carry):
        place = 2 * GROUP * index
        for half in range(2):
            here = place + half * GROUP
            for member in range(GROUP):
                exponents(here + 2 * GROUP + member, gaps[half][member])
                weigh(gaps[1 - half][member], weights[1 - half][member])
                add(here + member, weights[half][member])
        return carry

    return step


def facet_features(
    world_ref, own_ref, out_ref, push_ref, own_force, own_load,
    terms_ref, sem, table, listed, points, force_sum, load_sum, own_sem, *buffers,
):
    keeps = buffers[4 * GROUP + 2 :]
    copy = pltpu.make_async_copy(own_ref.at[pl.ds(48, 8), :], table, own_sem)
    copy.start()
    for keep in keeps:
        keep[...] = jnp.zeros(keep.shape, F32)

    def owner(index, terms_keep, push_keep):
        lever = [world_ref[index, part] for part in range(3)]
        normal = [world_ref[index, 3 + part] for part in range(3)]
        area = world_ref[index, 6]
        last = world_ref[index, 7]
        center = [
            jnp.clip(lever[part] + last[:, part : part + 1], -FAR, FAR) for part in range(3)
        ]
        along = normal[0] * center[0] + normal[1] * center[1] + normal[2] * center[2]
        square = center[0] * center[0] + center[1] * center[1] + center[2] * center[2]
        sides = (
            ([-SHARPNESS * value for value in normal], SHARPNESS * (CONTACT_GAP + along), 0.0),
            ([2.0 * value for value in center], -square, 1.0),
        )
        for side, (factors, constant, tail) in enumerate(sides):
            split = [split3(value) for value in factors]
            order = (0, 1, 2, 0, 1, 0)
            for group, level in enumerate(order):
                for part in range(3):
                    put(terms_keep, side * TERMS + 3 * group + part, split[part][level])
            for level, value in enumerate(split3(constant)):
                put(terms_keep, side * TERMS + 18 + level, value)
                put(terms_keep, side * TERMS + 21 + level, jnp.full((8, 128), tail, F32))
        scaled = (PENALTY / SHARPNESS) * area
        push = [scaled * value for value in normal]
        push.append(lever[1] * push[2] - lever[2] * push[1])
        push.append(lever[2] * push[0] - lever[0] * push[2])
        push.append(lever[0] * push[1] - lever[1] * push[0])
        for part in range(6):
            high = push[part].astype(BF16).astype(F32)
            put(push_keep, part, high)
            put(push_keep, 8 + part, push[part] - high)
        for block in range(BLOCKS):
            both = terms_keep[pl.ds(block, 2 * TERMS, stride=PITCH), :]
            terms_ref[index * BLOCKS + block, 0:128, :] = both[:TERMS].T.astype(BF16)
            terms_ref[index * BLOCKS + block, 128:256, :] = both[TERMS:].T.astype(BF16)
            push_ref[index * BLOCKS + block] = push_keep[
                pl.ds(block, 16, stride=PITCH), :
            ].astype(BF16)

    def owners(index, carry):
        for spare in range(SIDE):
            owner(SIDE * index + spare, *keeps[2 * spare : 2 * spare + 2])
        part = pl.ds(index * SIDE * BLOCKS, SIDE * BLOCKS)
        pltpu.make_async_copy(terms_ref.at[part], out_ref.at[part], sem).start()
        return carry

    lax.fori_loop(0, PLANE // SIDE, owners, 0)
    push_ref[FACETS] = jnp.zeros((16, 128), BF16)
    terms_ref[FACETS] = jnp.zeros((256, TERMS), BF16)
    points[BLOCKS] = jnp.zeros((TERMS, 256), BF16)
    force_sum[...] = jnp.zeros(force_sum.shape, F32)
    load_sum[...] = jnp.zeros(load_sum.shape, F32)
    copy.wait()
    particle_keep = buffers[4 * GROUP : 4 * GROUP + 2]
    for keep in particle_keep:
        keep[...] = jnp.zeros(keep.shape, F32)
    particle_terms(own_ref, points, 0, particle_keep)
    total = table[0, 127].astype(jnp.int32)

    def entry(step, carry):
        for spare in range(4):
            place = 4 * step + spare
            listed[2 * GROUP + place] = table[0, place].astype(jnp.int32)
        return carry

    lax.fori_loop(0, (total + 3) // 4, entry, 0)
    for spare in range(2 * GROUP):
        listed[spare] = BLOCKS * 256 + FACETS
    for spare in range(4 * GROUP):
        listed[2 * GROUP + total + spare] = BLOCKS * 256 + FACETS
    step = pipeline(terms_ref, push_ref, points, listed, force_sum, load_sum, buffers)
    lax.fori_loop(0, (total + 4 * GROUP - 1) // (2 * GROUP), step, 0)
    for block in range(BLOCKS):
        for part in range(3):
            own_force[8 * part + block : 8 * part + block + 1, :] = force_sum[
                block, part : part + 1, :
            ]
    own_load[...] = load_sum[0 : 2 * PLANE]
    done = pltpu.make_async_copy(terms_ref.at[pl.ds(0, FACETS)], out_ref, sem)
    done.wait()


def contact(
    held_ref, push_ref, given_ref, own_force, own_load, force_ref, load_ref,
    terms_ref, held_sem, table, listed, points, force_sum, load_sum,
    sem, *buffers,
):
    copy = pltpu.make_async_copy(given_ref.at[:, pl.ds(48, 8), :], table, sem)
    copy.start()
    held = []
    for part in range(4):
        place = pl.ds(ROW * part, ROW)
        held.append(
            pltpu.make_async_copy(held_ref.at[place], terms_ref.at[place], held_sem.at[part])
        )
        held[-1].start()
    terms_ref[FACETS] = jnp.zeros((256, TERMS), BF16)
    point_keeps = buffers[4 * GROUP :]
    for keep in point_keeps:
        keep[...] = jnp.zeros(keep.shape, F32)
    force_sum[...] = jnp.zeros(force_sum.shape, F32)
    load_sum[0 : 2 * PLANE] = own_load[...]
    load_sum[2 * PLANE] = jnp.zeros((8, 128), F32)
    plane = lax.axis_index("wide") // PLANE
    points[PARTICLES] = jnp.zeros((TERMS, 256), BF16)

    def sources(index, carry):
        for spare in range(SIDE):
            one = SIDE * index + spare
            keeps = point_keeps[2 * spare : 2 * spare + 2]
            particle_terms(given_ref.at[one], points, one * BLOCKS, keeps)
        return carry

    lax.fori_loop(0, DEPTH // SIDE, sources, 0)
    copy.wait()

    def gather(late, start):
        def one(index, start):
            early = table[index, 0, 126].astype(jnp.int32)
            first = jnp.where(late, early, 0)
            count = jnp.where(late, table[index, 0, 127].astype(jnp.int32) - early, early)
            count = jnp.where(index == plane, 0, count)
            shift = index * (BLOCKS * 256)

            def entry(step, carry):
                for spare in range(4):
                    place = 4 * step + spare
                    listed[start + place] = table[index, 0, first + place].astype(jnp.int32) + shift
                return carry

            lax.fori_loop(0, (count + 3) // 4, entry, 0)
            return start + count

        return lax.fori_loop(0, DEPTH, one, start)

    early = gather(False, 2 * GROUP)
    total = gather(True, early)
    for spare in range(2 * GROUP):
        listed[spare] = PARTICLES * 256 + FACETS
    for spare in range(4 * GROUP):
        listed[total + spare] = PARTICLES * 256 + FACETS

    step = pipeline(terms_ref, push_ref, points, listed, force_sum, load_sum, buffers)
    for one in held[:2]:
        one.wait()
    steps = (early - 2 * GROUP) // (2 * GROUP)
    lax.fori_loop(0, steps, step, 0)
    for one in held[2:]:
        one.wait()
    lax.fori_loop(steps, (total + 2 * GROUP - 1) // (2 * GROUP), step, 0)
    for index in range(DEPTH):
        for block in range(BLOCKS):
            for part in range(3):
                force_ref[index, 8 * part + block : 8 * part + block + 1, :] = force_sum[
                    index * BLOCKS + block, part : part + 1, :
                ]
    force_ref[plane] = own_force[...]
    load_ref[...] = load_sum[0 : 2 * PLANE]


def finish(
    force_ref, velocity_ref, mass_ref, own_ref, other_ref, pose_ref, spin_ref, out_ref, motion_ref,
):
    finish_boulders(own_ref, other_ref, pose_ref, spin_ref, motion_ref)
    total = force_ref[0]
    for index in range(1, DEPTH):
        total = total + force_ref[index]
    scaled = TIME_STEP * mass_ref[...]
    for part in range(3):
        out_ref[part] = velocity_ref[part] + scaled * total[8 * part : 8 * part + 8, :]


def finish_boulders(own_ref, other_ref, pose_ref, velocity_ref, out_ref):
    row = lax.broadcasted_iota(jnp.int32, (2, 6), 0)
    column = lax.broadcasted_iota(jnp.int32, (2, 6), 1)
    change = jnp.zeros((2, 6), F32)
    for boulder in range(2):
        pose = [pose_ref[boulder : boulder + 1, entry : entry + 1] for entry in range(16)]
        total = jnp.sum(own_ref[boulder] + other_ref[boulder], axis=1, keepdims=True)
        force = [-total[part : part + 1, :] for part in range(3)]
        torque = [-total[3 + part : 4 + part, :] for part in range(3)]
        moves = [pose[12] * value for value in force]
        body = []
        for part in range(3):
            turned = (
                pose[3 + part] * torque[0]
                + pose[6 + part] * torque[1]
                + pose[9 + part] * torque[2]
            )
            body.append(turned * pose[13 + part])
        for part in range(3):
            moves.append(
                pose[3 + 3 * part] * body[0]
                + pose[4 + 3 * part] * body[1]
                + pose[5 + 3 * part] * body[2]
            )
        for part in range(6):
            here = jnp.logical_and(row == boulder, column == part)
            change = change + jnp.where(here, moves[part], 0.0)
    out_ref[...] = velocity_ref[...] + TIME_STEP * change


VMEM = pl.BlockSpec(memory_space=pltpu.VMEM)
ANY = pl.BlockSpec(memory_space=pl.ANY)


def call(kernel, outs, in_specs, scratch=(), out_specs=VMEM, limit=VMEM_LIMIT):
    return pl.pallas_call(
        kernel,
        out_shape=outs,
        in_specs=in_specs,
        out_specs=out_specs,
        scratch_shapes=list(scratch),
        compiler_params=pltpu.CompilerParams(vmem_limit_bytes=limit),
    )


def shards(
    particle_position,
    particle_velocity,
    inverse_mass,
    facet_geometry,
    boulder_pose,
    boulder_velocity,
    boulder_slot,
    block_home,
    pair_facet,
    pair_block,
    pair_active,
):
    owners = lax.axis_size("wide")
    planes = [[PLANE * depth + spot for spot in range(PLANE)] for depth in range(owners // PLANE)]
    columns = [[PLANE * depth + spot for depth in range(DEPTH)] for spot in range(PLANE)]
    swap = functools.partial(
        lax.all_to_all, axis_name="wide", split_axis=0, concat_axis=0, tiled=True
    )
    pairs = pair_facet.shape[0]
    shape = jax.ShapeDtypeStruct

    def shift(step, unit):
        moves = []
        for device in range(owners):
            place = device // unit % 4
            moves.append((device, device + ((place + step) % 4 - place) * unit))
        return moves

    geometry = facet_geometry.transpose(0, 2, 1, 3)
    facets = call(
        facet_message,
        shape((PLANE, 8, BLOCKS, 128), F32),
        [ANY, ANY],
        [
            pltpu.VMEM(geometry.shape, F32),
            pltpu.SMEM(boulder_pose.shape, F32),
            pltpu.SemaphoreType.DMA((2,)),
        ],
        limit=WHOLE_VMEM,
    )(geometry, boulder_pose)
    facets = swap(facets, axis_index_groups=planes)
    lists = [
        particle_position.transpose(1, 0, 2),
        boulder_slot.reshape(-1, 128),
        block_home.reshape(-1, 128),
        pair_facet.reshape(1, pairs),
        pair_block.reshape(1, pairs),
        pair_active.reshape(1, pairs),
    ]
    particles, own = call(
        pair_message,
        [shape((DEPTH, 56, 128), F32), shape((56, 128), F32)],
        [ANY] * 6,
        [pltpu.VMEM(value.shape, value.dtype) for value in lists]
        + [pltpu.SemaphoreType.DMA((6,))],
        out_specs=[VMEM, VMEM],
        limit=WHOLE_VMEM,
    )(*lists)
    work = [pltpu.VMEM((256, 256), F32)] * (2 * GROUP) + [pltpu.VMEM((256, 256), BF16)] * (2 * GROUP)
    terms, push, own_force, own_load = call(
        facet_features,
        [
            shape((FACETS, 256, TERMS), BF16),
            shape((FACETS + 1, 16, 128), BF16),
            shape((24, 256), F32),
            shape((2 * PLANE, 8, 128), F32),
        ],
        [VMEM, VMEM],
        [
            pltpu.VMEM((FACETS + 1, 256, TERMS), BF16),
            pltpu.SemaphoreType.DMA,
            pltpu.SMEM((8, 128), F32),
            pltpu.SMEM((48 + 6 * GROUP,), jnp.int32),
            pltpu.VMEM((BLOCKS + 1, TERMS, 256), BF16),
            pltpu.VMEM((BLOCKS + 1, 8, 256), F32),
            pltpu.VMEM((2 * PLANE + 1, 8, 128), F32),
            pltpu.SemaphoreType.DMA,
        ]
        + work
        + [pltpu.VMEM((TERMS * PITCH, 128), F32)] * 2
        + [pltpu.VMEM((2 * TERMS * PITCH, 128), F32), pltpu.VMEM((16 * PITCH, 128), F32)] * SIDE,
        out_specs=[ANY, VMEM, VMEM, VMEM],
    )(facets, own)
    particles = swap(particles, axis_index_groups=columns)
    force, load = call(
        contact,
        [shape((DEPTH, 24, 256), F32), shape((2 * PLANE, 8, 128), F32)],
        [ANY] + [VMEM] * 4,
        [
            pltpu.VMEM((FACETS + 1, 256, TERMS), BF16),
            pltpu.SemaphoreType.DMA((4,)),
            pltpu.SMEM((DEPTH, 8, 128), F32),
            pltpu.SMEM((DEPTH * 48 + 6 * GROUP,), jnp.int32),
            pltpu.VMEM((PARTICLES + 1, TERMS, 256), BF16),
            pltpu.VMEM((PARTICLES + 1, 8, 256), F32),
            pltpu.VMEM((2 * PLANE + 1, 8, 128), F32),
            pltpu.SemaphoreType.DMA,
        ]
        + work
        + [pltpu.VMEM((TERMS * PITCH, 128), F32)] * (2 * SIDE),
        out_specs=[VMEM, VMEM],
    )(terms, push, particles, own_force, own_load)
    grid = load.reshape(4, 4, 2, 8, 128)
    spot = lax.axis_index("wide") % PLANE
    down, across = spot // 4, spot % 4
    def pick(array, axis, index):
        return lax.dynamic_index_in_dim(array, index % 4, axis, keepdims=False)

    row = pick(grid, 1, across)
    for step in (1, 2, 3):
        row = row + lax.ppermute(pick(grid, 1, across + step), "wide", shift(step, 1))
    load = pick(row, 0, down)
    for step in (1, 2, 3):
        load = load + lax.ppermute(pick(row, 0, down + step), "wide", shift(step, 4))
    other = lax.ppermute(load, "narrow", [(0, 1), (1, 0)])
    force = swap(force, axis_index_groups=columns)
    velocity = particle_velocity.transpose(1, 0, 2)
    new_velocity, boulder_motion = call(
        finish,
        [shape(velocity.shape, F32), shape(boulder_velocity.shape, F32)],
        [VMEM] * 7,
        out_specs=[VMEM, VMEM],
    )(force, velocity, inverse_mass, load, other, boulder_pose, boulder_velocity)
    return (new_velocity.transpose(1, 0, 2), boulder_motion)


def solution(mesh):
    return jax.shard_map(
        shards,
        mesh=mesh,
        in_specs=(
            P(("wide", "narrow"), None, None),
            P(("wide", "narrow"), None, None),
            P(("wide", "narrow"), None),
            P("wide", None, None, None),
            P("wide", None),
            P("wide", None),
            P(),
            P(),
            P(("wide", "narrow")),
            P(("wide", "narrow")),
            P(("wide", "narrow")),
        ),
        out_specs=(P(("wide", "narrow"), None, None), P("wide", None)),
        check_vma=False,
    )
```
